256 devices in a mesh: pair: 8 (over x, core), elem: 32 (over z, y).
Axes of the slice: x: 4, y: 4, z: 8, core: 2. Of those that a mesh axis runs over, the one named last changes fastest.
Arguments:
- gas_amounts: float32 [7, 24, 524288], P(None, None, ('pair', 'elem')), may hold values from 0.01 to 0.1
- layer_mass: float32 [24, 524288], P(None, ('pair', 'elem')), may hold values from 0.5 to 1.5
- cloud_paths: float32 [2, 24, 524288], P(None, None, ('pair', 'elem')), may hold values from 0 to 0.3
- surface_kind: int32 [524288], P(('pair', 'elem')), may hold values from 0 to 3
- snow_cover: float32 [524288], P(('pair', 'elem')), may hold values from 0 to 1
- snow_age: float32 [524288], P(('pair', 'elem')), may hold values from 0 to 1
- cos_zenith: float32 [524288], P(('pair', 'elem')), may hold values from 0.05 to 1
- sunlit: int32 [524288], P(('pair', 'elem')), may hold values from 0 to 1, as said below
- gas_coeff: float32 [7, 112], replicated, may hold values from 0.001 to 3
- rayleigh: float32 [112], replicated, may hold values from 0.001 to 0.05
- cloud_ext: float32 [2, 14], replicated, may hold values from 0.5 to 5
- surface_table: float32 [4, 14], replicated, may hold values from 0.03 to 0.6
- snow_table: float32 [14], replicated, may hold values from 0.5 to 0.95
- solar_weight: float32 [112], replicated, may hold values from 0.1 to 1
Outputs:
- heating: float32 [24, 524288], P(None, ('pair', 'elem'))
- surface_net: float32 [524288], P(('pair', 'elem'))
The draws below stay inside these ranges and needn't reach their ends.
Inputs may be any that keep to these rules, and one draw needn't show every extreme that they name: The columns at physics positions i and i + 262144 are never both sunlit.
All inputs are finite; a program needn't handle non-finite values.
Results may differ from the reference program's by a relative error of at most 0.0001.
Values sent between devices are 32-bit elements; how exact they have to be, the bound alone decides.
A program may use at most 192 MiB of HBM per device.

```python
import math
import jax
import jax.numpy as jnp
from jax import lax

G = 112
BANDS = 14
GASES = 7
LEVELS = 24
COL_DEV = 2048
PAIRS = 8
GROUPS = 32
COLS = 524288


def draw_sunlit(key, part):
    key = jax.random.fold_in(key, 7)
    key_roll, key_share = jax.random.split(key)
    half_pairs = PAIRS // 2
    random_roll = jax.random.randint(key_roll, (half_pairs, GROUPS, COL_DEV), 0, 1000)
    day_share = jax.random.randint(key_share, (half_pairs, GROUPS, 1), 0, 1001)
    day_share = day_share.at[0, 0, 0].set(1000)
    lower_lit = random_roll < day_share
    upper_lit = random_roll >= day_share + 100
    return jnp.concatenate([lower_lit, upper_lit], 0).astype(jnp.int32).reshape(-1)


def with_ends(array, stream_key, least, top_value):
    longest = array.shape.index(max(array.shape))
    spots = []
    for shift in (0, 1):
        where = [jax.random.randint(jax.random.fold_in(stream_key, axis), (), 0, length) for axis, length in enumerate(array.shape)]
        where[longest] = (where[longest] + shift) % array.shape[longest]
        spots.append(tuple(where))
    return array.at[spots[0]].set(least).at[spots[1]].set(top_value)


def block_levels(own_key, dims, pieces, smallest, largest):
    factor_of = 1.0
    for axis_at, parts in pieces:
        steps = jax.random.uniform(jax.random.fold_in(jax.random.fold_in(own_key, 6), axis_at), (parts,), jnp.float32, smallest / len(pieces), largest / len(pieces))
        factor_of = factor_of * jnp.repeat(jnp.exp(steps), dims[axis_at] // parts).reshape((-1,) + (1,) * (len(dims) - 1 - axis_at))
    return factor_of


def setup_inputs(seed: int = 0) -> dict:
    streams_of = jax.random.split(jax.random.key(seed), 15)
    gas_amounts = jnp.clip(jnp.exp(math.log(0.1) - 2.3025851 * jax.random.uniform(streams_of[0], (GASES, LEVELS, COLS), jnp.float32) ** block_levels(streams_of[0], (GASES, LEVELS, COLS), ((2, 256),), -0.2, 0.2)), 0.01, 0.1)
    layer_mass = jnp.clip(0.5 + 1.0 * jax.random.uniform(streams_of[1], (LEVELS, COLS), jnp.float32) ** block_levels(streams_of[1], (LEVELS, COLS), ((1, 256),), -0.2, 0.2), 0.5, 1.5)
    cloud_paths = jnp.clip(0.3 * jax.random.uniform(streams_of[2], (2, LEVELS, COLS), jnp.float32) ** block_levels(streams_of[2], (2, LEVELS, COLS), ((2, 256),), -0.2, 0.2), 0.0, 0.3)
    surface_kind = with_ends(jax.random.randint(streams_of[3], (COLS,), 0, 4), jax.random.fold_in(streams_of[3], 1), 0, 3).astype(jnp.int32)
    snow_cover = jnp.clip(1.0 * jax.random.uniform(streams_of[4], (COLS,), jnp.float32) ** block_levels(streams_of[4], (COLS,), ((0, 256),), -0.2, 0.2), 0.0, 1.0)
    snow_age = jnp.clip(1.0 * jax.random.uniform(streams_of[5], (COLS,), jnp.float32) ** block_levels(streams_of[5], (COLS,), ((0, 256),), -0.2, 0.2), 0.0, 1.0)
    cos_zenith = jnp.clip(0.05 + 0.95 * jax.random.uniform(streams_of[6], (COLS,), jnp.float32) ** block_levels(streams_of[6], (COLS,), ((0, 256),), -0.2, 0.2), 0.05, 1.0)
    sunlit = draw_sunlit(jax.random.fold_in(streams_of[14], 71), 0)
    gas_coeff = jnp.clip(jnp.exp(jax.random.uniform(streams_of[8], (GASES, G), jnp.float32, math.log(0.001), math.log(3.0))), 0.001, 3.0)
    rayleigh = jnp.clip(jnp.exp(jax.random.uniform(streams_of[9], (G,), jnp.float32, math.log(0.001), math.log(0.05))), 0.001, 0.05)
    cloud_ext = jnp.clip(jnp.exp(jax.random.uniform(streams_of[10], (2, BANDS), jnp.float32, math.log(0.5), math.log(5.0))), 0.5, 5.0)
    surface_table = jnp.clip(jax.random.uniform(streams_of[11], (4, BANDS), jnp.float32, 0.03, 0.6), 0.03, 0.6)
    snow_table = jnp.clip(jax.random.uniform(streams_of[12], (BANDS,), jnp.float32, 0.5, 0.95), 0.5, 0.95)
    solar_weight = jnp.clip(jnp.exp(jax.random.uniform(streams_of[13], (G,), jnp.float32, math.log(0.1), math.log(1.0))), 0.1, 1.0)
    return {"gas_amounts": gas_amounts, "layer_mass": layer_mass, "cloud_paths": cloud_paths, "surface_kind": surface_kind, "snow_cover": snow_cover, "snow_age": snow_age, "cos_zenith": cos_zenith, "sunlit": sunlit, "gas_coeff": gas_coeff, "rayleigh": rayleigh, "cloud_ext": cloud_ext, "surface_table": surface_table, "snow_table": snow_table, "solar_weight": solar_weight}


WATER_SSA = 0.999
ICE_SSA = 0.99
WATER_ASYM = 0.85
ICE_ASYM = 0.78
DIFFUSIVITY = 1.66


def regroup(values):
    leading = values.shape[:-1]
    per_group = COL_DEV // GROUPS
    shaped = values.reshape(leading + (PAIRS, GROUPS, GROUPS, per_group))
    shaped = jnp.swapaxes(shaped, -3, -2)
    return shaped.reshape(leading + (COLS,))


def surface_albedo(surface_kind, snow_cover, snow_age, surface_table, snow_table):
    kinds = jnp.arange(surface_table.shape[0], dtype=jnp.int32)
    onehot = (surface_kind[None, :] == kinds[:, None]).astype(jnp.float32)
    base_albedo = jnp.dot(surface_table.T, onehot, precision=lax.Precision.HIGHEST)
    snow_share = jnp.where(surface_kind >= 1, snow_cover, 0.0)
    fresh_snow = snow_table[:, None] * (1.0 - 0.5 * snow_age[None, :])
    return (1.0 - snow_share)[None, :] * base_albedo + snow_share[None, :] * fresh_snow


def optic_tables(gas_coeff, rayleigh, cloud_ext):
    gpt_count = gas_coeff.shape[1]
    cloud_gpt = jnp.repeat(cloud_ext, gpt_count // cloud_ext.shape[1], axis=1)
    gas_part = gas_coeff.T
    no_gas = jnp.zeros_like(gas_part)
    zero_col = jnp.zeros_like(rayleigh)
    extinct = jnp.concatenate([gas_part, jnp.stack([rayleigh, cloud_gpt[0], cloud_gpt[1]], 1)], 1)
    scatter = jnp.concatenate([no_gas, jnp.stack([rayleigh, WATER_SSA * cloud_gpt[0], ICE_SSA * cloud_gpt[1]], 1)], 1)
    forward = jnp.concatenate([no_gas, jnp.stack([zero_col, WATER_ASYM * WATER_SSA * cloud_gpt[0], ICE_ASYM * ICE_SSA * cloud_gpt[1]], 1)], 1)
    return jnp.concatenate([extinct, scatter, forward], 0)


def radiate(amounts, albedo_band, cos_zen, optic_stack, solar_frac):
    levels, fields, width = amounts.shape
    gpt_count = solar_frac.shape[0]
    combined = jnp.einsum("kf,lfw->lkw", optic_stack, amounts, precision=lax.Precision.HIGHEST)
    depth = combined[:, :gpt_count]
    scatter = combined[:, gpt_count:2 * gpt_count]
    forward = combined[:, 2 * gpt_count:]
    single = scatter / depth
    asymmetry = forward / scatter
    inv_cos = 1.0 / cos_zen
    diffuse_exp = jnp.exp(-DIFFUSIVITY * depth)
    beam_exp = jnp.exp(-depth * inv_cos[None, None, :])
    backward = 0.5 * single * (1.0 - asymmetry)
    onward = 0.5 * single * (1.0 + asymmetry)
    refl_diff = backward * (1.0 - diffuse_exp)
    tran_diff = diffuse_exp + onward * (1.0 - diffuse_exp)
    refl_dir = backward * (1.0 - beam_exp)
    scat_dir = onward * (1.0 - beam_exp)
    cum_depth = jnp.cumsum(depth, axis=0)
    depth_above = jnp.concatenate([jnp.zeros((1, gpt_count, width), jnp.float32), cum_depth], 0)
    direct = solar_frac[None, :, None] * cos_zen[None, None, :] * jnp.exp(-depth_above * inv_cos[None, None, :])
    ground_albedo = jnp.repeat(albedo_band, gpt_count // albedo_band.shape[0], axis=0)

    def upward(carried, inputs):
        alb_below, src_below = carried
        r_diff, t_diff, r_dir, s_dir, beam_top = inputs
        denom_inv = 1.0 / (1.0 - r_diff * alb_below)
        alb_here = r_diff + t_diff * t_diff * alb_below * denom_inv
        src_here = r_dir * beam_top + t_diff * denom_inv * (src_below + alb_below * s_dir * beam_top)
        return (alb_here, src_here), (alb_below, src_below, denom_inv)

    (alb_top, src_top), (alb_next, src_next, denoms) = lax.scan(
        upward, (ground_albedo, ground_albedo * direct[-1]),
        (refl_diff, tran_diff, refl_dir, scat_dir, direct[:-1]), reverse=True)
    net_top = direct[0] - src_top

    def downward(carried, inputs):
        down_flux, net_above = carried
        r_diff, t_diff, s_dir, beam_top, beam_bottom, alb_below, src_below, denom_inv = inputs
        down_below = (t_diff * down_flux + r_diff * src_below + s_dir * beam_top) * denom_inv
        up_below = alb_below * down_below + src_below
        net_below = down_below + beam_bottom - up_below
        return (down_below, net_below), jnp.sum(net_above - net_below, axis=0)

    (down_ground, net_ground), absorbed = lax.scan(
        downward, (jnp.zeros_like(net_top), net_top),
        (refl_diff, tran_diff, scat_dir, direct[:-1], direct[1:], alb_next, src_next, denoms))
    heat_rate = levels * absorbed / amounts[:, fields - 3, :]
    return heat_rate, jnp.sum(net_ground, axis=0)


def reference(gas_amounts, layer_mass, cloud_paths, surface_kind, snow_cover, snow_age, cos_zenith, sunlit,
              gas_coeff, rayleigh, cloud_ext, surface_table, snow_table, solar_weight):
    gases_phys = regroup(gas_amounts)
    mass_phys = regroup(layer_mass)
    amounts = jnp.concatenate([jnp.swapaxes(gases_phys, 0, 1), mass_phys[:, None, :],
                               jnp.swapaxes(cloud_paths, 0, 1)], 1)
    albedo_band = surface_albedo(surface_kind, snow_cover, snow_age, surface_table, snow_table)
    optic_stack = optic_tables(gas_coeff, rayleigh, cloud_ext)
    solar_frac = solar_weight / jnp.sum(solar_weight)
    block_width = min(COL_DEV, 512)
    blocks = COLS // block_width

    def one_block(block_index):
        start = block_index * block_width
        return radiate(lax.dynamic_slice_in_dim(amounts, start, block_width, 2),
                       lax.dynamic_slice_in_dim(albedo_band, start, block_width, 1),
                       lax.dynamic_slice_in_dim(cos_zenith, start, block_width, 0),
                       optic_stack, solar_frac)

    heat_blocks, flux_blocks = lax.map(one_block, jnp.arange(blocks, dtype=jnp.int32))
    heat_phys = jnp.swapaxes(heat_blocks, 0, 1).reshape(LEVELS, COLS)
    flux_phys = flux_blocks.reshape(COLS)
    lit_mask = sunlit == 1
    heating = regroup(jnp.where(lit_mask[None, :], heat_phys, 0.0))
    surface_net = jnp.where(lit_mask, flux_phys, 0.0)
    return heating, surface_net
```

```python
import functools

import jax
import jax.numpy as jnp
from jax import lax
from jax.experimental import pallas as pl
from jax.experimental.pallas import tpu as pltpu
from jax.sharding import PartitionSpec as P

WATER_SSA = 0.999
ICE_SSA = 0.99
WATER_ASYM = 0.85
ICE_ASYM = 0.78
DIFFUSIVITY = 1.66
LOG2E = 1.4426950408889634

F32 = jnp.float32
BF16 = jnp.bfloat16
LANES = 128
HALF = 64
GPTS = 112
BANDS = 14
LEVELS = 24
GASES = 7
FIELD_ROWS = 8 * LEVELS
PACKED_ROWS = FIELD_ROWS // 2
STATE_ROWS = 56
STEPS = 8
UNROLL = 24
MESH = pl.DeviceIdType.MESH


def split3(x):
    first = x.astype(BF16).astype(F32)
    rest = x - first
    second = rest.astype(BF16).astype(F32)
    return first, second, rest - second


def lane_pad(x):
    return jnp.concatenate([x, jnp.zeros((x.shape[0], LANES - x.shape[1]), F32)], 1)


def make_tables(gas, ray, cloud, solar, surface, snow, coef_ref, solar_ref, albtab_ref):
    shape = (BANDS, LANES)
    band = lax.broadcasted_iota(jnp.int32, shape, 1) // 8 == lax.broadcasted_iota(jnp.int32, shape, 0)
    cloud_gpt = jnp.dot(
        cloud, band.astype(F32), precision=lax.Precision.HIGHEST, preferred_element_type=F32
    )
    ray = lane_pad(ray)
    water, ice = WATER_SSA * cloud_gpt[0:1], ICE_SSA * cloud_gpt[1:2]
    zero6, zero7, zero32 = (jnp.zeros((n, LANES), F32) for n in (6, 7, 32))
    stacks = (
        [lane_pad(gas), ray, cloud_gpt, zero6],
        [zero7, 0.5 * ray, 0.5 * (1 - WATER_ASYM) * water, 0.5 * (1 - ICE_ASYM) * ice, zero6],
        [zero7, 0.5 * ray, 0.5 * (1 + WATER_ASYM) * water, 0.5 * (1 + ICE_ASYM) * ice, zero6],
    )
    for index, stack in enumerate(stacks):
        a1, a2, a3 = split3(jnp.concatenate(stack, 0))
        terms = jnp.concatenate([a1, a1, a2, a1, a3, a2, zero32], 0)
        coef_ref[pl.ds(index * GPTS, GPTS), :] = jnp.transpose(terms)[:GPTS].astype(BF16)
    solar = lane_pad(solar)
    solar = solar / jnp.sum(solar)
    square = (LANES, LANES)
    solar_ref[...] = jnp.transpose(jnp.broadcast_to(solar, square))[:GPTS]
    rows = jnp.concatenate([lane_pad(surface), lane_pad(snow)], 0)
    for index in range(5):
        albtab_ref[pl.ds(index * 16, 16), :] = jnp.transpose(
            jnp.broadcast_to(rows[index : index + 1], square)
        )[:16]


def compute_tile(x_ref, state, coef_ref, solar_ref, albtab_ref, alb_ref, layer_ref, net_ref):
    block = (8, LANES)
    kind, share, age, cosine = state[0:1], state[1:2], state[2:3], state[3:4]
    beam_scale = jnp.broadcast_to(-LOG2E / cosine, block)
    base = jnp.zeros((16, LANES), F32)
    for index in range(4):
        base = jnp.where(kind == float(index), albtab_ref[pl.ds(index * 16, 16), :], base)
    fresh = albtab_ref[pl.ds(64, 16), :] * (1.0 - 0.5 * age)
    alb_ref[...] = (1.0 - share) * base + share * fresh

    def upward(step, carried):
        alb, src = carried
        layer = LEVELS - 1 - step
        x1, x2, x3 = split3(x_ref[pl.ds(layer, 16, stride=LEVELS), :])
        terms = jnp.concatenate([x1, x2, x1, x3, x1, x2, jnp.zeros((32, LANES), F32)], 0)
        optics = jnp.dot(coef_ref[...], terms.astype(BF16), preferred_element_type=F32)
        next_alb, next_src = [], []
        for b in range(BANDS):
            depth = optics[8 * b : 8 * b + 8]
            inv_depth = pl.reciprocal(depth, approx=True)
            backward = optics[GPTS + 8 * b : GPTS + 8 * b + 8] * inv_depth
            onward = optics[2 * GPTS + 8 * b : 2 * GPTS + 8 * b + 8] * inv_depth
            diffuse_exp = jnp.exp2(depth * (-DIFFUSIVITY * LOG2E))
            beam_exp = jnp.exp2(depth * beam_scale)
            diffuse_loss = 1.0 - diffuse_exp
            beam_loss = 1.0 - beam_exp
            refl_diff = backward * diffuse_loss
            tran_diff = diffuse_exp + onward * diffuse_loss
            refl_dir = backward * beam_loss
            scat_dir = onward * beam_loss
            denom = pl.reciprocal(1.0 - refl_diff * alb[b], approx=True)
            through = tran_diff * denom
            src_beam = src[b] * beam_exp
            gain = (refl_diff * src_beam + scat_dir) * denom
            src_here = refl_dir + through * (src_beam + alb[b] * scat_dir)
            alb_here = refl_diff + tran_diff * through * alb[b]
            layer_ref[layer, 0, b] = through
            layer_ref[layer, 1, b] = gain
            layer_ref[layer, 2, b] = beam_exp
            layer_ref[layer, 3, b] = 1.0 - alb_here
            layer_ref[layer, 4, b] = 1.0 - src_here
            next_alb.append(alb_here)
            next_src.append(src_here)
        return tuple(next_alb), tuple(next_src)

    ground = tuple(jnp.broadcast_to(alb_ref[b : b + 1, :], block) for b in range(BANDS))
    lax.fori_loop(0, LEVELS, upward, (ground, ground), unroll=UNROLL)

    def downward(layer, carried):
        down, direct = carried
        net = jnp.zeros(block, F32)
        next_down, next_direct = [], []
        for b in range(BANDS):
            net = net + (layer_ref[layer, 3, b] * down[b] + layer_ref[layer, 4, b] * direct[b])
            next_down.append(layer_ref[layer, 0, b] * down[b] + layer_ref[layer, 1, b] * direct[b])
            next_direct.append(layer_ref[layer, 2, b] * direct[b])
        net_ref[layer] = net
        return tuple(next_down), tuple(next_direct)

    beam = tuple(solar_ref[pl.ds(8 * b, 8), :] * cosine for b in range(BANDS))
    none = tuple(jnp.zeros(block, F32) for b in range(BANDS))
    down, direct = lax.fori_loop(0, LEVELS, downward, (none, beam), unroll=UNROLL)
    net = jnp.zeros(block, F32)
    for b in range(BANDS):
        net = net + (1.0 - jnp.broadcast_to(alb_ref[b : b + 1, :], block)) * (down[b] + direct[b])
    net_ref[LEVELS] = net
    nets = jnp.sum(net_ref[...], axis=1)
    mass = x_ref[pl.ds(GASES * LEVELS, LEVELS), :]
    return float(LEVELS) * (nets[:LEVELS] - nets[1:]) / mass, nets[LEVELS:]


def kernel(
    gas_ref, mass_ref, cloud_ref, kind_ref, cover_ref, age_ref, cosine_ref, lit_ref,
    coeff_ref, ray_ref, cext_ref, surface_ref, snow_ref, weight_ref,
    heat_ref, flux_ref,
    send, recv, state, their_state, result, returned, flux_out, flux_in,
    x_ref, coef_ref, solar_ref, albtab_ref, alb_ref, layer_ref, net_ref,
    send_sem, recv_sem, state_send, state_recv, result_send, result_recv, fluxo_sem, fluxi_sem,
):
    pair, elem = lax.axis_index("pair"), lax.axis_index("elem")
    half_pairs = lax.axis_size("pair") // 2
    side, group = pair // half_pairs, pair % half_pairs
    z, y = elem // 4, elem % 4
    y_pair, y_low = y // 2, y % 2
    other = 1 - side
    partner = (other * half_pairs + group, elem)

    def device(which_side, which_elem):
        return (which_side * half_pairs + group, which_elem)

    barrier = pltpu.get_barrier_semaphore()

    def greet_other(k, _):
        pl.semaphore_signal(barrier, inc=1, device_id=device(other, k), device_id_type=MESH)
        return 0

    def greet_own(index, _):
        k = ((z + 2 * (index // 4) + side) % 8) * 4 + index % 4

        @pl.when(k != elem)
        def _():
            pl.semaphore_signal(barrier, inc=1, device_id=device(side, k), device_id_type=MESH)

        return 0

    lax.fori_loop(0, 32, greet_other, 0)
    lax.fori_loop(0, 16, greet_own, 0)

    for tile in range(16):
        state[tile, 0:48, :] = cloud_ref[:, tile * LANES : (tile + 1) * LANES]
        kind = kind_ref[tile : tile + 1, :]
        state[tile, 48:49, :] = kind.astype(F32)
        state[tile, 49:50, :] = jnp.where(kind >= 1, cover_ref[tile : tile + 1, :], 0.0)
        state[tile, 50:51, :] = age_ref[tile : tile + 1, :]
        state[tile, 51:52, :] = cosine_ref[tile : tile + 1, :]
        state[tile, 52:53, :] = lit_ref[tile : tile + 1, :].astype(F32)
        state[tile, 53:56, :] = jnp.zeros((3, LANES), F32)
    x_ref[...] = jnp.zeros_like(x_ref)

    pl.semaphore_wait(barrier, 47 + side)

    low_half = lax.broadcasted_iota(jnp.int32, (PACKED_ROWS, LANES), 1) < HALF
    low_half8 = lax.broadcasted_iota(jnp.int32, (8, LANES), 1) < HALF
    low_half24 = lax.broadcasted_iota(jnp.int32, (LEVELS, LANES), 1) < HALF

    def tile_of(step, which_side, sign):
        z_step = 2 * (step // 2) + which_side
        return ((z + 8 + sign * z_step) % 8) * 2 + (y_pair + step % 2) % 2

    def gas_copy(step, which_side, k):
        return pltpu.make_async_remote_copy(
            src_ref=send.at[k],
            dst_ref=recv.at[side, step, y_low],
            send_sem=send_sem.at[k],
            recv_sem=recv_sem.at[side, step, y_low],
            device_id=device(which_side, k),
            device_id_type=MESH,
        )

    def send_gas(index, _):
        step, which_side = index // 2, index % 2
        tile = tile_of(step, which_side, 1)
        columns = pl.ds(pl.multiple_of(tile * LANES, LANES), LANES)
        first = gas_ref[0:PACKED_ROWS, columns]
        second = jnp.concatenate([gas_ref[PACKED_ROWS : GASES * LEVELS, columns], mass_ref[:, columns]], 0)
        send[2 * tile] = jnp.where(low_half, first, pltpu.roll(second, HALF, 1))
        send[2 * tile + 1] = jnp.where(low_half, pltpu.roll(first, HALF, 1), second)
        for low in range(2):
            k = 2 * tile + low
            local = jnp.logical_and(which_side == side, k == elem)

            @pl.when(jnp.logical_not(local))
            def _():
                gas_copy(step, which_side, k).start()

            @pl.when(local)
            def _():
                pltpu.make_async_copy(
                    send.at[k], recv.at[side, step, y_low], recv_sem.at[side, step, y_low]
                ).start()

        return 0

    def state_copy(step):
        return pltpu.make_async_remote_copy(
            src_ref=state.at[tile_of(step, other, -1)],
            dst_ref=their_state.at[step],
            send_sem=state_send.at[step],
            recv_sem=state_recv.at[step],
            device_id=partner,
            device_id_type=MESH,
        )

    def send_state(step, _):
        state_copy(step).start()
        return 0

    lax.fori_loop(0, 4, send_gas, 0)
    lax.fori_loop(0, STEPS, send_state, 0)
    lax.fori_loop(4, 16, send_gas, 0)

    make_tables(
        coeff_ref[...], ray_ref[...], cext_ref[...], weight_ref[...], surface_ref[...], snow_ref[...],
        coef_ref, solar_ref, albtab_ref,
    )

    def result_copy(step, which_side, low):
        element = 2 * tile_of(step, side, -1) + low
        return element, pltpu.make_async_remote_copy(
            src_ref=result.at[step, which_side, (low + y_low) % 2],
            dst_ref=returned.at[elem],
            send_sem=result_send.at[step, which_side, low],
            recv_sem=result_recv.at[elem],
            device_id=device(which_side, element),
            device_id_type=MESH,
        )

    def flux_copy(step):
        return pltpu.make_async_remote_copy(
            src_ref=flux_out.at[step],
            dst_ref=flux_in.at[step],
            send_sem=fluxo_sem.at[step],
            recv_sem=fluxi_sem.at[step],
            device_id=partner,
            device_id_type=MESH,
        )

    def both_halves(row):
        row = jnp.broadcast_to(row, (8, LANES))
        turned = pltpu.roll(row, HALF, 1)
        return jnp.where(low_half8, row, turned)[0:1], jnp.where(low_half8, turned, row)[0:1]

    def one_tile(step, _):
        tile = tile_of(step, side, -1)
        state_copy(step).wait_recv()
        for which_side in range(2):
            for low in range(2):
                pltpu.make_async_copy(
                    recv.at[which_side, step, low],
                    recv.at[which_side, step, low],
                    recv_sem.at[which_side, step, low],
                ).wait()
        mine, theirs = state[tile], their_state[step]
        own_lit, other_lit = mine[52:53], theirs[52:53]
        merged = jnp.where(own_lit > 0.5, mine, theirs)
        mask0, mask1 = both_halves(own_lit)
        part0 = jnp.where(mask0 > 0.5, recv[side, step, 0], recv[other, step, 0])
        part1 = jnp.where(mask1 > 0.5, recv[side, step, 1], recv[other, step, 1])
        x_ref[pl.ds(0, PACKED_ROWS), :] = jnp.where(low_half, part0, pltpu.roll(part1, HALF, 1))
        x_ref[pl.ds(PACKED_ROWS, PACKED_ROWS), :] = jnp.where(low_half, pltpu.roll(part0, HALF, 1), part1)
        x_ref[pl.ds(FIELD_ROWS, 2 * LEVELS), :] = merged[0 : 2 * LEVELS]
        heat, flux = compute_tile(
            x_ref, merged[2 * LEVELS :], coef_ref, solar_ref, albtab_ref, alb_ref, layer_ref, net_ref
        )
        flux_ref[pl.ds(tile, 1), :] = jnp.where(own_lit > 0.5, flux, 0.0)
        flux_out[step] = jnp.broadcast_to(jnp.where(other_lit > 0.5, flux, 0.0), (8, LANES))
        flux_copy(step).start()
        for which_side in range(2):
            lit = jnp.where(which_side == side, own_lit, other_lit) > 0.5
            kept = jnp.where(lit, heat, 0.0)
            result[step, which_side, 0] = kept
            result[step, which_side, 1] = pltpu.roll(kept, HALF, 1)
            for low in range(2):
                element, copy = result_copy(step, which_side, low)
                local = jnp.logical_and(which_side == side, element == elem)

                @pl.when(jnp.logical_not(local))
                def _():
                    copy.start()

                @pl.when(local)
                def _():
                    pltpu.make_async_copy(
                        result.at[step, which_side, (low + y_low) % 2],
                        returned.at[elem],
                        result_recv.at[elem],
                    ).start()

        return 0

    lax.fori_loop(0, STEPS, one_tile, 0)

    def finish_flux(step, _):
        flux_copy(step).wait()
        flux_ref[pl.ds(tile_of(step, other, -1), 1), :] = flux_in[step, 0:1, :]
        state_copy(step).wait_send()
        for which_side in range(2):
            for low in range(2):
                element, copy = result_copy(step, which_side, low)
                local = jnp.logical_and(which_side == side, element == elem)

                @pl.when(jnp.logical_not(local))
                def _():
                    copy.wait_send()

        return 0

    def finish_gas(index, _):
        step, which_side = index // 2, index % 2
        tile = tile_of(step, which_side, 1)
        for low in range(2):
            k = 2 * tile + low
            local = jnp.logical_and(which_side == side, k == elem)

            @pl.when(jnp.logical_not(local))
            def _():
                gas_copy(step, which_side, k).wait_send()

        return 0

    def finish_heat(tile, _):
        for low in range(2):
            pltpu.make_async_copy(
                returned.at[2 * tile + low], returned.at[2 * tile + low], result_recv.at[2 * tile + low]
            ).wait()
        columns = pl.ds(pl.multiple_of(tile * LANES, LANES), LANES)
        heat_ref[:, columns] = jnp.where(low_half24, returned[2 * tile], returned[2 * tile + 1])
        return 0

    lax.fori_loop(0, 16, finish_gas, 0)
    lax.fori_loop(0, STEPS, finish_flux, 0)
    lax.fori_loop(0, 16, finish_heat, 0)


def body(
    gas_amounts, layer_mass, cloud_paths, surface_kind, snow_cover, snow_age, cos_zenith, sunlit,
    gas_coeff, rayleigh, cloud_ext, surface_table, snow_table, solar_weight,
):
    width = layer_mass.shape[1]
    rows = lambda x: x.reshape(width // LANES, LANES)
    vmem = pl.BlockSpec(memory_space=pltpu.VMEM)
    dma = pltpu.SemaphoreType.DMA
    heating, flux = pl.pallas_call(
        kernel,
        out_shape=(
            jax.ShapeDtypeStruct((LEVELS, width), F32),
            jax.ShapeDtypeStruct((width // LANES, LANES), F32),
        ),
        in_specs=[vmem] * 14,
        out_specs=(vmem, vmem),
        scratch_shapes=[
            pltpu.VMEM((32, PACKED_ROWS, LANES), F32),
            pltpu.VMEM((2, STEPS, 2, PACKED_ROWS, LANES), F32),
            pltpu.VMEM((16, STATE_ROWS, LANES), F32),
            pltpu.VMEM((STEPS, STATE_ROWS, LANES), F32),
            pltpu.VMEM((STEPS, 2, 2, LEVELS, LANES), F32),
            pltpu.VMEM((32, LEVELS, LANES), F32),
            pltpu.VMEM((STEPS, 8, LANES), F32),
            pltpu.VMEM((STEPS, 8, LANES), F32),
            pltpu.VMEM((16 * LEVELS, LANES), F32),
            pltpu.VMEM((3 * GPTS, LANES), BF16),
            pltpu.VMEM((GPTS, LANES), F32),
            pltpu.VMEM((80, LANES), F32),
            pltpu.VMEM((16, LANES), F32),
            pltpu.VMEM((LEVELS, 5, BANDS, 8, LANES), F32),
            pltpu.VMEM((LEVELS + 1, 8, LANES), F32),
            dma((32,)),
            dma((2, STEPS, 2)),
            dma((STEPS,)),
            dma((STEPS,)),
            dma((STEPS, 2, 2)),
            dma((32,)),
            dma((STEPS,)),
            dma((STEPS,)),
        ],
        compiler_params=pltpu.CompilerParams(
            collective_id=0, has_side_effects=True, vmem_limit_bytes=40 * 2**20
        ),
    )(
        gas_amounts.reshape(GASES * LEVELS, width),
        layer_mass,
        cloud_paths.reshape(2 * LEVELS, width),
        rows(surface_kind), rows(snow_cover), rows(snow_age), rows(cos_zenith), rows(sunlit),
        gas_coeff, rayleigh.reshape(1, GPTS), cloud_ext, surface_table,
        snow_table.reshape(1, BANDS), solar_weight.reshape(1, GPTS),
    )
    return heating, flux.reshape(width)


def solution(mesh):
    columns = ("pair", "elem")
    placed = (
        P(None, None, columns), P(None, columns), P(None, None, columns),
        P(columns), P(columns), P(columns), P(columns), P(columns),
        P(), P(), P(), P(), P(), P(),
    )
    return jax.shard_map(
        body,
        mesh=mesh,
        in_specs=placed,
        out_specs=(P(None, columns), P(columns)),
        check_vma=False,
    )
```

```python
import functools

import jax
import jax.numpy as jnp
from jax import lax
from jax.experimental import pallas as pl
from jax.experimental.pallas import tpu as pltpu
from jax.sharding import PartitionSpec as P

WATER_SSA = 0.999
ICE_SSA = 0.99
WATER_ASYM = 0.85
ICE_ASYM = 0.78
DIFFUSIVITY = 1.66
LOG2E = 1.4426950408889634

F32 = jnp.float32
BF16 = jnp.bfloat16
LANES = 128
HALF = 64
GPTS = 112
BANDS = 14
LEVELS = 24
GASES = 7
FIELD_ROWS = 8 * LEVELS
CLOUD_ROWS = 2 * LEVELS
STATE_ROWS = 56
PACKED_ROWS = 32
LIT_ROW = 20
STEPS = 8
TILES = 16
UNROLL = 24
MESH = pl.DeviceIdType.MESH
SPACE = pltpu.HBM


def split3(x):
    first = x.astype(BF16).astype(F32)
    rest = x - first
    second = rest.astype(BF16).astype(F32)
    return first, second, rest - second


def lane_pad(x):
    return jnp.concatenate([x, jnp.zeros((x.shape[0], LANES - x.shape[1]), F32)], 1)


def make_tables(gas, ray, cloud, solar, surface, snow, coef_ref, solar_ref, albtab_ref):
    shape = (BANDS, LANES)
    band = lax.broadcasted_iota(jnp.int32, shape, 1) // 8 == lax.broadcasted_iota(jnp.int32, shape, 0)
    cloud_gpt = jnp.dot(
        cloud, band.astype(F32), precision=lax.Precision.HIGHEST, preferred_element_type=F32
    )
    ray = lane_pad(ray)
    water, ice = WATER_SSA * cloud_gpt[0:1], ICE_SSA * cloud_gpt[1:2]
    zero6, zero7, zero32 = (jnp.zeros((n, LANES), F32) for n in (6, 7, 32))
    stacks = (
        [lane_pad(gas), ray, cloud_gpt, zero6],
        [zero7, 0.5 * ray, 0.5 * (1 - WATER_ASYM) * water, 0.5 * (1 - ICE_ASYM) * ice, zero6],
        [zero7, 0.5 * ray, 0.5 * (1 + WATER_ASYM) * water, 0.5 * (1 + ICE_ASYM) * ice, zero6],
    )
    for index, stack in enumerate(stacks):
        a1, a2, a3 = split3(jnp.concatenate(stack, 0))
        terms = jnp.concatenate([a1, a1, a2, a1, a3, a2, zero32], 0)
        coef_ref[pl.ds(index * GPTS, GPTS), :] = jnp.transpose(terms)[:GPTS].astype(BF16)
    solar = lane_pad(solar)
    solar = solar / jnp.sum(solar)
    square = (LANES, LANES)
    solar_ref[...] = jnp.transpose(jnp.broadcast_to(solar, square))[:GPTS]
    rows = jnp.concatenate([lane_pad(surface), lane_pad(snow)], 0)
    for index in range(5):
        albtab_ref[pl.ds(index * 16, 16), :] = jnp.transpose(
            jnp.broadcast_to(rows[index : index + 1], square)
        )[:16]


def compute_tile(x_ref, state, coef_ref, solar_ref, albtab_ref, alb_ref, layer_ref, net_ref):
    block = (8, LANES)
    kind, share, age, cosine = state[0:1], state[1:2], state[2:3], state[3:4]
    beam_scale = jnp.broadcast_to(-LOG2E / cosine, block)
    base = jnp.zeros((16, LANES), F32)
    for index in range(4):
        base = jnp.where(kind == float(index), albtab_ref[pl.ds(index * 16, 16), :], base)
    fresh = albtab_ref[pl.ds(64, 16), :] * (1.0 - 0.5 * age)
    alb_ref[...] = (1.0 - share) * base + share * fresh

    def upward(step, carried):
        alb, src = carried
        layer = LEVELS - 1 - step
        x1, x2, x3 = split3(x_ref[pl.ds(layer, 16, stride=LEVELS), :])
        terms = jnp.concatenate([x1, x2, x1, x3, x1, x2, jnp.zeros((32, LANES), F32)], 0)
        optics = jnp.dot(coef_ref[...], terms.astype(BF16), preferred_element_type=F32)
        next_alb, next_src = [], []
        for b in range(BANDS):
            depth = optics[8 * b : 8 * b + 8]
            inv_depth = pl.reciprocal(depth, approx=True)
            backward = optics[GPTS + 8 * b : GPTS + 8 * b + 8] * inv_depth
            onward = optics[2 * GPTS + 8 * b : 2 * GPTS + 8 * b + 8] * inv_depth
            diffuse_exp = jnp.exp2(depth * (-DIFFUSIVITY * LOG2E))
            beam_exp = jnp.exp2(depth * beam_scale)
            diffuse_loss = 1.0 - diffuse_exp
            beam_loss = 1.0 - beam_exp
            refl_diff = backward * diffuse_loss
            tran_diff = diffuse_exp + onward * diffuse_loss
            refl_dir = backward * beam_loss
            scat_dir = onward * beam_loss
            denom = pl.reciprocal(1.0 - refl_diff * alb[b], approx=True)
            through = tran_diff * denom
            src_beam = src[b] * beam_exp
            gain = (refl_diff * src_beam + scat_dir) * denom
            src_here = refl_dir + through * (src_beam + alb[b] * scat_dir)
            alb_here = refl_diff + tran_diff * through * alb[b]
            layer_ref[layer, 0, b] = through
            layer_ref[layer, 1, b] = gain
            layer_ref[layer, 2, b] = beam_exp
            layer_ref[layer, 3, b] = 1.0 - alb_here
            layer_ref[layer, 4, b] = 1.0 - src_here
            next_alb.append(alb_here)
            next_src.append(src_here)
        return tuple(next_alb), tuple(next_src)

    ground = tuple(jnp.broadcast_to(alb_ref[b : b + 1, :], block) for b in range(BANDS))
    lax.fori_loop(0, LEVELS, upward, (ground, ground), unroll=UNROLL)

    def downward(layer, carried):
        down, direct = carried
        net = jnp.zeros(block, F32)
        next_down, next_direct = [], []
        for b in range(BANDS):
            net = net + (layer_ref[layer, 3, b] * down[b] + layer_ref[layer, 4, b] * direct[b])
            next_down.append(layer_ref[layer, 0, b] * down[b] + layer_ref[layer, 1, b] * direct[b])
            next_direct.append(layer_ref[layer, 2, b] * direct[b])
        net_ref[layer] = net
        return tuple(next_down), tuple(next_direct)

    beam = tuple(solar_ref[pl.ds(8 * b, 8), :] * cosine for b in range(BANDS))
    none = tuple(jnp.zeros(block, F32) for b in range(BANDS))
    down, direct = lax.fori_loop(0, LEVELS, downward, (none, beam), unroll=UNROLL)
    net = jnp.zeros(block, F32)
    for b in range(BANDS):
        net = net + (1.0 - jnp.broadcast_to(alb_ref[b : b + 1, :], block)) * (down[b] + direct[b])
    net_ref[LEVELS] = net
    nets = jnp.sum(net_ref[...], axis=1)
    mass = x_ref[pl.ds(GASES * LEVELS, LEVELS), :]
    return float(LEVELS) * (nets[:LEVELS] - nets[1:]) / mass, nets[LEVELS:]


def kernel(
    gas_hbm, mass_hbm, cloud_hbm, kind_hbm, cover_hbm, age_hbm, cosine_hbm, lit_hbm,
    coeff_hbm, ray_hbm, cext_hbm, surface_hbm, snow_hbm, weight_hbm,
    heat_ref, flux_ref,
    gas_own, mass_own, cloud_ref, kind_ref, cover_ref, age_ref, cosine_ref, lit_ref,
    coeff_ref, ray_ref, cext_ref, surface_ref, snow_ref, weight_ref,
    gas_in, mass_in, send, recv, heat_out, flux_out, flux_in,
    x_ref, coef_ref, solar_ref, albtab_ref, alb_ref, layer_ref, net_ref,
    load_sem, own_sem, gas_send, gas_recv, mass_send, mass_recv,
    state_send, state_recv, heat_send, heat_recv, flux_send, flux_recv,
):
    pair, elem = lax.axis_index("pair"), lax.axis_index("elem")
    half_pairs = lax.axis_size("pair") // 2
    side, group = pair // half_pairs, pair % half_pairs
    z, y = elem // 4, elem % 4
    z_block, z_odd, y_pair, y_low = z // 2, z % 2, y // 2, y % 2
    other = 1 - side

    def device(which_side, which_elem):
        return (which_side * half_pairs + group, which_elem)

    partner = device(other, elem)

    def columns(tile):
        return pl.ds(pl.multiple_of(tile * LANES, LANES), LANES)

    def step_tile(step, which_side):
        return 2 * (2 * ((z_block + step // 2) % 4) + which_side) + (y_pair + step % 2) % 2

    def own_copies(step):
        tile = columns(step_tile(step, side))
        return (
            pltpu.make_async_copy(gas_hbm.at[:, tile], gas_own.at[step], own_sem.at[0, step]),
            pltpu.make_async_copy(mass_hbm.at[:, tile], mass_own.at[step], own_sem.at[1, step]),
        )

    state_loads = [
        pltpu.make_async_copy(source, target, load_sem.at[index])
        for index, (source, target) in enumerate((
            (cloud_hbm, cloud_ref), (kind_hbm, kind_ref), (cover_hbm, cover_ref),
            (age_hbm, age_ref), (cosine_hbm, cosine_ref), (lit_hbm, lit_ref),
        ))
    ]
    table_loads = [
        pltpu.make_async_copy(source, target, load_sem.at[6 + index])
        for index, (source, target) in enumerate((
            (coeff_hbm, coeff_ref), (ray_hbm, ray_ref), (cext_hbm, cext_ref),
            (surface_hbm, surface_ref), (snow_hbm, snow_ref), (weight_hbm, weight_ref),
        ))
    ]

    barrier = pltpu.get_barrier_semaphore()

    def greet(which_side, k):
        @pl.when(jnp.logical_or(which_side != side, k != elem))
        def _():
            pl.semaphore_signal(barrier, inc=1, device_id=device(which_side, k), device_id_type=MESH)

    def greet_all(k, _):
        greet(z_odd, k)
        return 0

    def greet_some(index, _):
        greet(1 - z_odd, (2 * (index // 4) + side) * 4 + index % 4)
        return 0

    lax.fori_loop(0, 32, greet_all, 0)
    lax.fori_loop(0, 16, greet_some, 0)

    for copy in state_loads + table_loads:
        copy.start()

    def load_own(step, _):
        for copy in own_copies(step):
            copy.start()
        return 0

    lax.fori_loop(0, STEPS, load_own, 0)

    low_packed = lax.broadcasted_iota(jnp.int32, (PACKED_ROWS, LANES), 1) < HALF
    low8 = lax.broadcasted_iota(jnp.int32, (8, LANES), 1) < HALF

    for copy in state_loads:
        copy.wait()

    for tile in range(TILES):
        row = slice(tile, tile + 1)
        kind = kind_ref[row, :]
        share = jnp.where(kind >= 1, cover_ref[row, :], 0.0)
        first = cloud_ref[0:PACKED_ROWS, tile * LANES : (tile + 1) * LANES]
        second = jnp.concatenate(
            [
                cloud_ref[PACKED_ROWS:CLOUD_ROWS, tile * LANES : (tile + 1) * LANES],
                kind.astype(F32), share, age_ref[row, :], cosine_ref[row, :], lit_ref[row, :].astype(F32),
                jnp.zeros((11, LANES), F32),
            ],
            0,
        )
        send[2 * tile] = jnp.where(low_packed, first, pltpu.roll(second, HALF, 1))
        send[2 * tile + 1] = jnp.where(low_packed, pltpu.roll(first, HALF, 1), second)

    for copy in table_loads:
        copy.wait()
    make_tables(
        coeff_ref[...], ray_ref[...], cext_ref[...], weight_ref[...], surface_ref[...], snow_ref[...],
        coef_ref, solar_ref, albtab_ref,
    )
    x_ref[...] = jnp.zeros_like(x_ref)

    pl.semaphore_wait(barrier, 48 - jnp.where(side == z_odd, 1, 0))

    def gas_copies(step):
        tile = columns(step_tile(step, other))
        return (
            pltpu.make_async_remote_copy(
                src_ref=gas_hbm.at[:, tile], dst_ref=gas_in.at[step],
                send_sem=gas_send.at[step], recv_sem=gas_recv.at[step],
                device_id=partner, device_id_type=MESH,
            ),
            pltpu.make_async_remote_copy(
                src_ref=mass_hbm.at[:, tile], dst_ref=mass_in.at[step],
                send_sem=mass_send.at[step], recv_sem=mass_recv.at[step],
                device_id=partner, device_id_type=MESH,
            ),
        )

    def for_states(step, remote, local=None):
        for z_low in range(2):
            z_to = 2 * ((z_block + 4 - step // 2) % 4) + z_low
            for low in range(2):
                k = 4 * z_to + 2 * ((y_pair + step % 2) % 2) + low
                here = jnp.logical_and(z_odd == side, k == elem)

                @pl.when(jnp.logical_not(here))
                def _():
                    remote(
                        pltpu.make_async_remote_copy(
                            src_ref=send.at[k], dst_ref=recv.at[side, step, y_low],
                            send_sem=state_send.at[k], recv_sem=state_recv.at[side, step, y_low],
                            device_id=device(z_odd, k), device_id_type=MESH,
                        )
                    )

                if local is not None:
                    @pl.when(here)
                    def _():
                        local(
                            pltpu.make_async_copy(
                                send.at[k], recv.at[side, step, y_low], state_recv.at[side, step, y_low]
                            )
                        )

    def send_step(step, _):
        for copy in gas_copies(step):
            copy.start()
        for_states(step, lambda copy: copy.start(), lambda copy: copy.start())
        return 0

    lax.fori_loop(0, STEPS, send_step, 0)

    def heat_copy(step):
        return pltpu.make_async_remote_copy(
            src_ref=heat_out.at[step], dst_ref=heat_ref.at[:, columns(step_tile(step, side))],
            send_sem=heat_send.at[step], recv_sem=heat_recv.at[step],
            device_id=partner, device_id_type=MESH,
        )

    def for_fluxes(step, remote, local=None):
        for which_side in range(2):
            for low in range(2):
                k = 2 * step_tile(step, side) + low
                source = flux_out.at[step, which_side, (low + y_low) % 2]
                here = jnp.logical_and(which_side == side, k == elem)

                @pl.when(jnp.logical_not(here))
                def _():
                    remote(
                        pltpu.make_async_remote_copy(
                            src_ref=source, dst_ref=flux_in.at[elem],
                            send_sem=flux_send.at[step, which_side, low], recv_sem=flux_recv.at[elem],
                            device_id=device(which_side, k), device_id_type=MESH,
                        )
                    )

                if local is not None:
                    @pl.when(here)
                    def _():
                        local(pltpu.make_async_copy(source, flux_in.at[elem], flux_recv.at[elem]))

    def one_tile(step, _):
        for copy in own_copies(step):
            copy.wait()
        for which_side in range(2):
            for low in range(2):
                block = recv.at[which_side, step, low]
                pltpu.make_async_copy(block, block, state_recv.at[which_side, step, low]).wait()
        for copy in gas_copies(step):
            copy.wait_recv()
        own0, own1 = recv[side, step, 0], recv[side, step, 1]
        other0, other1 = recv[other, step, 0], recv[other, step, 1]

        def lit_masks(block0, block1):
            row0, row1 = block0[16:24], block1[16:24]
            turned0, turned1 = pltpu.roll(row0, HALF, 1), pltpu.roll(row1, HALF, 1)
            at = slice(LIT_ROW - 16, LIT_ROW - 15)
            return (
                jnp.where(low8, turned0, row0)[at] > 0.5,
                jnp.where(low8, turned1, row1)[at] > 0.5,
                jnp.where(low8, turned0, row1)[at] > 0.5,
            )

        mask0, mask1, own_lit = lit_masks(own0, own1)
        other_lit = lit_masks(other0, other1)[2]
        part0 = jnp.where(mask0, own0, other0)
        part1 = jnp.where(mask1, own1, other1)
        first = jnp.where(low_packed, part0, pltpu.roll(part1, HALF, 1))
        second = jnp.where(low_packed, pltpu.roll(part0, HALF, 1), part1)
        gas_rows = GASES * LEVELS
        x_ref[pl.ds(0, gas_rows), :] = jnp.where(own_lit, gas_own[step], gas_in[step])
        x_ref[pl.ds(gas_rows, LEVELS), :] = jnp.where(own_lit, mass_own[step], mass_in[step])
        x_ref[pl.ds(FIELD_ROWS, PACKED_ROWS), :] = first
        x_ref[pl.ds(FIELD_ROWS + PACKED_ROWS, CLOUD_ROWS - PACKED_ROWS), :] = second[0 : CLOUD_ROWS - PACKED_ROWS]
        heat, flux = compute_tile(
            x_ref, second[16:24], coef_ref, solar_ref, albtab_ref, alb_ref, layer_ref, net_ref
        )
        heat_out[step] = jnp.where(other_lit, heat, 0.0)
        heat_copy(step).start()
        for which_side in range(2):
            lit = jnp.where(which_side == side, own_lit.astype(F32), other_lit.astype(F32)) > 0.5
            kept = jnp.broadcast_to(jnp.where(lit, flux, 0.0), (8, LANES))
            flux_out[step, which_side, 0] = kept[0:1]
            flux_out[step, which_side, 1] = pltpu.roll(kept, HALF, 1)[0:1]
        for_fluxes(step, lambda copy: copy.start(), lambda copy: copy.start())
        heat_ref[:, columns(step_tile(step, side))] = jnp.where(own_lit, heat, 0.0)
        return 0

    lax.fori_loop(0, STEPS, one_tile, 0)

    def finish(step, _):
        for copy in gas_copies(step):
            copy.wait_send()
        for_states(step, lambda copy: copy.wait_send())
        for_fluxes(step, lambda copy: copy.wait_send())
        heat_copy(step).wait()
        return 0

    def finish_flux(tile, _):
        for low in range(2):
            row = flux_in.at[2 * tile + low]
            pltpu.make_async_copy(row, row, flux_recv.at[2 * tile + low]).wait()
        flux_ref[pl.ds(tile, 1), :] = jnp.where(low8[0:1], flux_in[2 * tile], flux_in[2 * tile + 1])
        return 0

    lax.fori_loop(0, STEPS, finish, 0)
    lax.fori_loop(0, TILES, finish_flux, 0)


def body(
    gas_amounts, layer_mass, cloud_paths, surface_kind, snow_cover, snow_age, cos_zenith, sunlit,
    gas_coeff, rayleigh, cloud_ext, surface_table, snow_table, solar_weight,
):
    width = layer_mass.shape[1]
    rows = lambda x: x.reshape(width // LANES, LANES)
    dma = pltpu.SemaphoreType.DMA
    hbm = pl.BlockSpec(memory_space=SPACE)
    vmem = pl.BlockSpec(memory_space=pltpu.VMEM)
    wide = lambda *lead: pltpu.VMEM(lead + (LANES,), F32)
    heating, flux = pl.pallas_call(
        kernel,
        out_shape=(
            jax.ShapeDtypeStruct((LEVELS, width), F32),
            jax.ShapeDtypeStruct((width // LANES, LANES), F32),
        ),
        in_specs=[hbm] * 14,
        out_specs=(vmem, vmem),
        scratch_shapes=[
            wide(STEPS, GASES * LEVELS), wide(STEPS, LEVELS), pltpu.VMEM((CLOUD_ROWS, width), F32),
            pltpu.VMEM((TILES, LANES), jnp.int32), wide(TILES), wide(TILES), wide(TILES),
            pltpu.VMEM((TILES, LANES), jnp.int32),
            pltpu.VMEM((GASES, GPTS), F32), pltpu.VMEM((1, GPTS), F32), pltpu.VMEM((2, BANDS), F32),
            pltpu.VMEM((4, BANDS), F32), pltpu.VMEM((1, BANDS), F32), pltpu.VMEM((1, GPTS), F32),
            wide(STEPS, GASES * LEVELS), wide(STEPS, LEVELS),
            wide(32, PACKED_ROWS), wide(2, STEPS, 2, PACKED_ROWS),
            wide(STEPS, LEVELS), wide(STEPS, 2, 2, 1), wide(32, 1),
            wide(16 * LEVELS), pltpu.VMEM((3 * GPTS, LANES), BF16), wide(GPTS), wide(80), wide(16),
            wide(LEVELS, 5, BANDS, 8), wide(LEVELS + 1, 8),
            dma((12,)), dma((2, STEPS)), dma((STEPS,)), dma((STEPS,)), dma((STEPS,)), dma((STEPS,)),
            dma((32,)), dma((2, STEPS, 2)), dma((STEPS,)), dma((STEPS,)), dma((STEPS, 2, 2)), dma((32,)),
        ],
        compiler_params=pltpu.CompilerParams(
            collective_id=0, has_side_effects=True, vmem_limit_bytes=60 * 2**20
        ),
    )(
        gas_amounts.reshape(GASES * LEVELS, width),
        layer_mass,
        cloud_paths.reshape(CLOUD_ROWS, width),
        rows(surface_kind), rows(snow_cover), rows(snow_age), rows(cos_zenith), rows(sunlit),
        gas_coeff, rayleigh.reshape(1, GPTS), cloud_ext, surface_table,
        snow_table.reshape(1, BANDS), solar_weight.reshape(1, GPTS),
    )
    return heating, flux.reshape(width)


def solution(mesh):
    columns = ("pair", "elem")
    placed = (
        P(None, None, columns), P(None, columns), P(None, None, columns),
        P(columns), P(columns), P(columns), P(columns), P(columns),
        P(), P(), P(), P(), P(), P(),
    )
    return jax.shard_map(
        body,
        mesh=mesh,
        in_specs=placed,
        out_specs=(P(None, columns), P(columns)),
        check_vma=False,
    )
```

```python
import functools

import jax
import jax.numpy as jnp
from jax import lax
from jax.experimental import pallas as pl
from jax.experimental.pallas import tpu as pltpu
from jax.sharding import PartitionSpec as P

WATER_SSA = 0.999
ICE_SSA = 0.99
WATER_ASYM = 0.85
ICE_ASYM = 0.78
DIFFUSIVITY = 1.66
LOG2E = 1.4426950408889634

F32 = jnp.float32
BF16 = jnp.bfloat16
LANES = 128
HALF = 64
GPTS = 112
BANDS = 14
LEVELS = 24
GASES = 7
FIELD_ROWS = 8 * LEVELS
CLOUD_ROWS = 2 * LEVELS
GAS_ROWS = GASES * LEVELS
PACKED_ROWS = 32
SENT_ROWS = 28
AHEAD = 3
STEPS = 8
TILES = 16
UNROLL = 24
MESH = pl.DeviceIdType.MESH
SPACE = pltpu.HBM


def split3(x):
    first = x.astype(BF16).astype(F32)
    rest = x - first
    second = rest.astype(BF16).astype(F32)
    return first, second, rest - second


def lane_pad(x):
    return jnp.concatenate([x, jnp.zeros((x.shape[0], LANES - x.shape[1]), F32)], 1)


def make_tables(gas, ray, cloud, solar, surface, snow, coef_ref, solar_ref, albtab_ref):
    shape = (BANDS, LANES)
    band = lax.broadcasted_iota(jnp.int32, shape, 1) // 8 == lax.broadcasted_iota(jnp.int32, shape, 0)
    cloud_gpt = jnp.dot(
        cloud, band.astype(F32), precision=lax.Precision.HIGHEST, preferred_element_type=F32
    )
    ray = lane_pad(ray)
    water, ice = WATER_SSA * cloud_gpt[0:1], ICE_SSA * cloud_gpt[1:2]
    zero6, zero7, zero32 = (jnp.zeros((n, LANES), F32) for n in (6, 7, 32))
    stacks = (
        [lane_pad(gas), ray, cloud_gpt, zero6],
        [zero7, 0.5 * ray, 0.5 * (1 - WATER_ASYM) * water, 0.5 * (1 - ICE_ASYM) * ice, zero6],
        [zero7, 0.5 * ray, 0.5 * (1 + WATER_ASYM) * water, 0.5 * (1 + ICE_ASYM) * ice, zero6],
    )
    for index, stack in enumerate(stacks):
        a1, a2, a3 = split3(jnp.concatenate(stack, 0) * (-DIFFUSIVITY * LOG2E))
        terms = jnp.concatenate([a1, a1, a2, a1, a3, a2, zero32], 0)
        coef_ref[pl.ds(index * GPTS, GPTS), :] = jnp.transpose(terms)[:GPTS].astype(BF16)
    solar = lane_pad(solar)
    solar = solar / jnp.sum(solar)
    square = (LANES, LANES)
    solar_ref[...] = jnp.transpose(jnp.broadcast_to(solar, square))[:GPTS]
    rows = jnp.concatenate([lane_pad(surface), lane_pad(snow)], 0)
    for index in range(5):
        albtab_ref[pl.ds(index * 16, 16), :] = jnp.transpose(
            jnp.broadcast_to(rows[index : index + 1], square)
        )[:16]


def compute_tile(x_ref, state, coef_ref, solar_ref, albtab_ref, alb_ref, layer_ref, net_ref):
    block = (8, LANES)
    kind, share, age, cosine = state[0:1], state[1:2], state[2:3], state[3:4]
    beam_scale = jnp.broadcast_to((1.0 / DIFFUSIVITY) / cosine, block)
    base = jnp.zeros((16, LANES), F32)
    for index in range(4):
        base = jnp.where(kind == float(index), albtab_ref[pl.ds(index * 16, 16), :], base)
    fresh = albtab_ref[pl.ds(64, 16), :] * (1.0 - 0.5 * age)
    alb_ref[...] = (1.0 - share) * base + share * fresh

    def upward(step, carried):
        alb, src = carried
        layer = LEVELS - 1 - step
        x1, x2, x3 = split3(x_ref[pl.ds(layer, 16, stride=LEVELS), :])
        terms = jnp.concatenate([x1, x2, x1, x3, x1, x2, jnp.zeros((32, LANES), F32)], 0)
        optics = jnp.dot(coef_ref[...], terms.astype(BF16), preferred_element_type=F32)
        next_alb, next_src = [], []
        for b in range(BANDS):
            depth = optics[8 * b : 8 * b + 8]
            inv_depth = pl.reciprocal(depth, approx=True)
            backward = optics[GPTS + 8 * b : GPTS + 8 * b + 8] * inv_depth
            onward = optics[2 * GPTS + 8 * b : 2 * GPTS + 8 * b + 8] * inv_depth
            diffuse_exp = jnp.exp2(depth)
            beam_exp = jnp.exp2(depth * beam_scale)
            diffuse_loss = 1.0 - diffuse_exp
            beam_loss = 1.0 - beam_exp
            refl_diff = backward * diffuse_loss
            tran_diff = diffuse_exp + onward * diffuse_loss
            refl_dir = backward * beam_loss
            scat_dir = onward * beam_loss
            denom = pl.reciprocal(1.0 - refl_diff * alb[b], approx=True)
            through = tran_diff * denom
            src_beam = src[b] * beam_exp
            gain = (refl_diff * src_beam + scat_dir) * denom
            src_here = refl_dir + through * (src_beam + alb[b] * scat_dir)
            alb_here = refl_diff + tran_diff * through * alb[b]
            layer_ref[layer, 0, b] = through
            layer_ref[layer, 1, b] = gain
            layer_ref[layer, 2, b] = beam_exp
            layer_ref[layer, 3, b] = 1.0 - alb_here
            layer_ref[layer, 4, b] = 1.0 - src_here
            next_alb.append(alb_here)
            next_src.append(src_here)
        return tuple(next_alb), tuple(next_src)

    ground = tuple(jnp.broadcast_to(alb_ref[b : b + 1, :], block) for b in range(BANDS))
    lax.fori_loop(0, LEVELS, upward, (ground, ground), unroll=UNROLL)

    def downward(layer, carried):
        down, direct = carried
        nets, next_down, next_direct = [], [], []
        for b in range(BANDS):
            nets.append(layer_ref[layer, 3, b] * down[b] + layer_ref[layer, 4, b] * direct[b])
            next_down.append(layer_ref[layer, 0, b] * down[b] + layer_ref[layer, 1, b] * direct[b])
            next_direct.append(layer_ref[layer, 2, b] * direct[b])
        while len(nets) > 1:
            nets = [sum(nets[i : i + 2][1:], nets[i]) for i in range(0, len(nets), 2)]
        net_ref[layer] = nets[0]
        return tuple(next_down), tuple(next_direct)

    beam = tuple(solar_ref[pl.ds(8 * b, 8), :] * cosine for b in range(BANDS))
    none = tuple(jnp.zeros(block, F32) for b in range(BANDS))
    down, direct = lax.fori_loop(0, LEVELS, downward, (none, beam), unroll=UNROLL)
    net = jnp.zeros(block, F32)
    for b in range(BANDS):
        net = net + (1.0 - jnp.broadcast_to(alb_ref[b : b + 1, :], block)) * (down[b] + direct[b])
    net_ref[LEVELS] = net
    nets = jnp.sum(net_ref[...], axis=1)
    mass = x_ref[pl.ds(GASES * LEVELS, LEVELS), :]
    return float(LEVELS) * (nets[:LEVELS] - nets[1:]) / mass, nets[LEVELS:]


def kernel(
    gas_hbm, mass_hbm, cloud_hbm, kind_hbm, cover_hbm, age_hbm, cosine_hbm, lit_hbm,
    coeff_hbm, ray_hbm, cext_hbm, surface_hbm, snow_hbm, weight_hbm,
    heat_ref, flux_ref,
    gas_own, cloud_ref, kind_ref, cover_ref, age_ref, cosine_ref, lit_ref,
    coeff_ref, ray_ref, cext_ref, surface_ref, snow_ref, weight_ref,
    gas_in, send, recv, heat_out, flux_out, flux_in,
    x_ref, coef_ref, solar_ref, albtab_ref, alb_ref, layer_ref, net_ref,
    load_sem, own_sem, gas_send, gas_recv,
    state_send, state_recv, heat_send, heat_recv, flux_send, flux_recv,
):
    pair, elem = lax.axis_index("pair"), lax.axis_index("elem")
    half_pairs = lax.axis_size("pair") // 2
    side, group = pair // half_pairs, pair % half_pairs
    z, y = elem // 4, elem % 4
    z_block, z_odd, y_pair, y_low = z // 2, z % 2, y // 2, y % 2
    other = 1 - side
    some_local = z_odd == side

    def device(which_side, which_elem):
        return (which_side * half_pairs + group, which_elem)

    partner = device(other, elem)

    def columns(tile):
        return pl.ds(pl.multiple_of(tile * LANES, LANES), LANES)

    def wait_bytes(ref, sem):
        pltpu.make_async_copy(ref, ref, sem).wait()

    def step_tile(step, which_side):
        return 2 * (2 * ((z_block + step // 2) % 4) + which_side) + (y_pair + step % 2) % 2

    state_loads = [
        pltpu.make_async_copy(source, target, load_sem.at[index])
        for index, (source, target) in enumerate((
            (cloud_hbm, cloud_ref), (kind_hbm, kind_ref), (cover_hbm, cover_ref),
            (age_hbm, age_ref), (cosine_hbm, cosine_ref), (lit_hbm, lit_ref),
        ))
    ]
    table_loads = [
        pltpu.make_async_copy(source, target, load_sem.at[6 + index])
        for index, (source, target) in enumerate((
            (coeff_hbm, coeff_ref), (ray_hbm, ray_ref), (cext_hbm, cext_ref),
            (surface_hbm, surface_ref), (snow_hbm, snow_ref), (weight_hbm, weight_ref),
        ))
    ]
    for copy in state_loads:
        copy.start()

    barrier = pltpu.get_barrier_semaphore()

    def greet(which_side, k):
        @pl.when(jnp.logical_or(which_side != side, k != elem))
        def _():
            pl.semaphore_signal(barrier, inc=1, device_id=device(which_side, k), device_id_type=MESH)

    def greet_all(k, _):
        greet(z_odd, k)
        return 0

    def greet_some(index, _):
        greet(1 - z_odd, (2 * (index // 4) + side) * 4 + index % 4)
        return 0

    lax.fori_loop(0, 32, greet_all, 0)
    lax.fori_loop(0, 16, greet_some, 0)

    for copy in table_loads:
        copy.start()

    def load_own(step, _):
        tile = columns(step_tile(step, side))
        pltpu.make_async_copy(
            gas_hbm.at[:, tile], gas_own.at[step, pl.ds(0, GAS_ROWS)], own_sem.at[step]
        ).start()
        pltpu.make_async_copy(
            mass_hbm.at[:, tile], gas_own.at[step, pl.ds(GAS_ROWS, LEVELS)], own_sem.at[step]
        ).start()
        return 0

    lax.fori_loop(0, STEPS, load_own, 0)

    low_packed = lax.broadcasted_iota(jnp.int32, (PACKED_ROWS, LANES), 1) < HALF
    low8 = lax.broadcasted_iota(jnp.int32, (8, LANES), 1) < HALF

    for copy in state_loads:
        copy.wait()

    def sent_tile(step, z_low):
        z_to = 2 * ((z_block + 4 - step // 2) % 4) + z_low
        return 2 * z_to + (y_pair + step % 2) % 2

    def pack_step(step, _):
        for z_low in range(2):
            tile = sent_tile(step, z_low)
            row = pl.ds(tile, 1)
            kind = kind_ref[row, :]
            share = jnp.where(kind >= 1, cover_ref[row, :], 0.0)
            first = jnp.concatenate(
                [
                    cloud_ref[0:LEVELS, columns(tile)], kind.astype(F32), share,
                    age_ref[row, :], cosine_ref[row, :], jnp.zeros((4, LANES), F32),
                ],
                0,
            )
            second = jnp.concatenate(
                [
                    cloud_ref[LEVELS:CLOUD_ROWS, columns(tile)], lit_ref[row, :].astype(F32),
                    jnp.zeros((7, LANES), F32),
                ],
                0,
            )
            send[2 * tile] = jnp.where(low_packed, first, pltpu.roll(second, HALF, 1))
            send[2 * tile + 1] = jnp.where(low_packed, pltpu.roll(first, HALF, 1), second)
        return 0

    lax.fori_loop(0, AHEAD, pack_step, 0)

    pl.semaphore_wait(barrier, 48 - jnp.where(some_local, 1, 0))

    sent = pl.ds(0, SENT_ROWS)

    def send_step(step, _):
        tile = columns(step_tile(step, other))
        for source, target in (
            (gas_hbm.at[:, tile], gas_in.at[step, pl.ds(0, GAS_ROWS)]),
            (mass_hbm.at[:, tile], gas_in.at[step, pl.ds(GAS_ROWS, LEVELS)]),
        ):
            pltpu.make_async_remote_copy(
                src_ref=source, dst_ref=target, send_sem=gas_send, recv_sem=gas_recv.at[step],
                device_id=partner, device_id_type=MESH,
            ).start()
        for z_low in range(2):
            for low in range(2):
                k = 2 * sent_tile(step, z_low) + low
                here = jnp.logical_and(some_local, k == elem)
                source, target = send.at[k, sent], recv.at[step, side, y_low, sent]

                @pl.when(jnp.logical_not(here))
                def _():
                    pltpu.make_async_remote_copy(
                        src_ref=source, dst_ref=target, send_sem=state_send, recv_sem=state_recv.at[step],
                        device_id=device(z_odd, k), device_id_type=MESH,
                    ).start()

                @pl.when(here)
                def _():
                    pltpu.make_async_copy(source, target, state_recv.at[step]).start()

        return 0

    lax.fori_loop(0, AHEAD, send_step, 0)
    lax.fori_loop(AHEAD, STEPS, pack_step, 0)
    for copy in table_loads:
        copy.wait()
    make_tables(
        coeff_ref[...], ray_ref[...], cext_ref[...], weight_ref[...], surface_ref[...], snow_ref[...],
        coef_ref, solar_ref, albtab_ref,
    )
    x_ref[pl.ds(10 * LEVELS, 6 * LEVELS), :] = jnp.zeros((6 * LEVELS, LANES), F32)

    def one_tile(step, _):
        tile = step_tile(step, side)
        wait_bytes(gas_own.at[step], own_sem.at[step])
        wait_bytes(recv.at[step, :, :, sent], state_recv.at[step])
        wait_bytes(gas_in.at[step], gas_recv.at[step])

        @pl.when(step + AHEAD < STEPS)
        def _():
            send_step(step + AHEAD, 0)

        own0, own1 = recv[step, side, 0], recv[step, side, 1]
        other0, other1 = recv[step, other, 0], recv[step, other, 1]

        def lit_masks(block0, block1):
            row0, row1 = block0[LEVELS:], block1[LEVELS:]
            turned0, turned1 = pltpu.roll(row0, HALF, 1), pltpu.roll(row1, HALF, 1)
            return (
                jnp.where(low8, turned0, row0)[0:1] > 0.5,
                jnp.where(low8, turned1, row1)[0:1] > 0.5,
                jnp.where(low8, turned0, row1)[0:1] > 0.5,
            )

        mask0, mask1, own_lit = lit_masks(own0, own1)
        other_lit = lit_masks(other0, other1)[2]
        part0 = jnp.where(mask0, own0, other0)
        part1 = jnp.where(mask1, own1, other1)
        first = jnp.where(low_packed, part0, pltpu.roll(part1, HALF, 1))
        second = jnp.where(low_packed, pltpu.roll(part0, HALF, 1), part1)
        x_ref[pl.ds(0, FIELD_ROWS), :] = jnp.where(own_lit, gas_own[step], gas_in[step])
        x_ref[pl.ds(FIELD_ROWS, LEVELS), :] = first[0:LEVELS]
        x_ref[pl.ds(FIELD_ROWS + LEVELS, LEVELS), :] = second[0:LEVELS]
        heat, flux = compute_tile(
            x_ref, first[LEVELS:], coef_ref, solar_ref, albtab_ref, alb_ref, layer_ref, net_ref
        )
        for which_side in range(2):
            lit = jnp.where(which_side == side, own_lit.astype(F32), other_lit.astype(F32)) > 0.5
            kept = jnp.broadcast_to(jnp.where(lit, flux, 0.0), (8, LANES))
            flux_out[step, which_side, 0] = kept[0:1]
            flux_out[step, which_side, 1] = pltpu.roll(kept, HALF, 1)[0:1]
        for which_side in range(2):
            for low in range(2):
                k = 2 * tile + low
                here = jnp.logical_and(which_side == side, k == elem)
                source, target = flux_out.at[step, which_side, (low + y_low) % 2], flux_in.at[elem]

                @pl.when(jnp.logical_not(here))
                def _():
                    pltpu.make_async_remote_copy(
                        src_ref=source, dst_ref=target, send_sem=flux_send, recv_sem=flux_recv,
                        device_id=device(which_side, k), device_id_type=MESH,
                    ).start()

                @pl.when(here)
                def _():
                    pltpu.make_async_copy(source, target, flux_recv).start()

        heat_out[step] = jnp.where(other_lit, heat, 0.0)
        pltpu.make_async_remote_copy(
            src_ref=heat_out.at[step], dst_ref=heat_ref.at[:, columns(tile)],
            send_sem=heat_send, recv_sem=heat_recv,
            device_id=partner, device_id_type=MESH,
        ).start()
        heat_ref[:, columns(tile)] = jnp.where(own_lit, heat, 0.0)
        return 0

    lax.fori_loop(0, STEPS, one_tile, 0)

    wait_bytes(gas_in, gas_send)

    @pl.when(some_local)
    def _():
        wait_bytes(send.at[pl.ds(0, 31), sent], state_send)
        wait_bytes(flux_in.at[pl.ds(0, 31)], flux_send)

    @pl.when(jnp.logical_not(some_local))
    def _():
        wait_bytes(send.at[:, sent], state_send)
        wait_bytes(flux_in, flux_send)

    wait_bytes(heat_out, heat_send)
    wait_bytes(flux_in, flux_recv)
    for tile in range(TILES):
        flux_ref[tile : tile + 1, :] = jnp.where(low8[0:1], flux_in[2 * tile], flux_in[2 * tile + 1])
    wait_bytes(heat_out, heat_recv)


def body(
    gas_amounts, layer_mass, cloud_paths, surface_kind, snow_cover, snow_age, cos_zenith, sunlit,
    gas_coeff, rayleigh, cloud_ext, surface_table, snow_table, solar_weight,
):
    width = layer_mass.shape[1]
    rows = lambda x: x.reshape(width // LANES, LANES)
    dma = pltpu.SemaphoreType.DMA
    hbm = pl.BlockSpec(memory_space=SPACE)
    vmem = pl.BlockSpec(memory_space=pltpu.VMEM)
    wide = lambda *lead: pltpu.VMEM(lead + (LANES,), F32)
    heating, flux = pl.pallas_call(
        kernel,
        out_shape=(
            jax.ShapeDtypeStruct((LEVELS, width), F32),
            jax.ShapeDtypeStruct((width // LANES, LANES), F32),
        ),
        in_specs=[hbm] * 14,
        out_specs=(vmem, vmem),
        scratch_shapes=[
            wide(STEPS, FIELD_ROWS), pltpu.VMEM((CLOUD_ROWS, width), F32),
            pltpu.VMEM((TILES, LANES), jnp.int32), wide(TILES), wide(TILES), wide(TILES),
            pltpu.VMEM((TILES, LANES), jnp.int32),
            pltpu.VMEM((GASES, GPTS), F32), pltpu.VMEM((1, GPTS), F32), pltpu.VMEM((2, BANDS), F32),
            pltpu.VMEM((4, BANDS), F32), pltpu.VMEM((1, BANDS), F32), pltpu.VMEM((1, GPTS), F32),
            wide(STEPS, FIELD_ROWS), wide(32, PACKED_ROWS), wide(STEPS, 2, 2, PACKED_ROWS),
            wide(STEPS, LEVELS), wide(STEPS, 2, 2, 1), wide(32, 1),
            wide(16 * LEVELS), pltpu.VMEM((3 * GPTS, LANES), BF16), wide(GPTS), wide(80), wide(16),
            wide(LEVELS, 5, BANDS, 8), wide(LEVELS + 1, 8),
            dma((12,)), dma((STEPS,)), dma, dma((STEPS,)),
            dma, dma((STEPS,)), dma, dma, dma, dma,
        ],
        compiler_params=pltpu.CompilerParams(
            collective_id=0, has_side_effects=True, vmem_limit_bytes=60 * 2**20
        ),
    )(
        gas_amounts.reshape(GASES * LEVELS, width),
        layer_mass,
        cloud_paths.reshape(CLOUD_ROWS, width),
        rows(surface_kind), rows(snow_cover), rows(snow_age), rows(cos_zenith), rows(sunlit),
        gas_coeff, rayleigh.reshape(1, GPTS), cloud_ext, surface_table,
        snow_table.reshape(1, BANDS), solar_weight.reshape(1, GPTS),
    )
    return heating, flux.reshape(width)


def solution(mesh):
    columns = ("pair", "elem")
    placed = (
        P(None, None, columns), P(None, columns), P(None, None, columns),
        P(columns), P(columns), P(columns), P(columns), P(columns),
        P(), P(), P(), P(), P(), P(),
    )
    return jax.shard_map(
        body,
        mesh=mesh,
        in_specs=placed,
        out_specs=(P(None, columns), P(columns)),
        check_vma=False,
    )
```

```python
import functools

import jax
import jax.numpy as jnp
from jax import lax
from jax.experimental import pallas as pl
from jax.experimental.pallas import tpu as pltpu
from jax.sharding import PartitionSpec as P

WATER_SSA = 0.999
ICE_SSA = 0.99
WATER_ASYM = 0.85
ICE_ASYM = 0.78
DIFFUSIVITY = 1.66
LOG2E = 1.4426950408889634

F32 = jnp.float32
BF16 = jnp.bfloat16
LANES = 128
HALF = 64
GPTS = 112
BANDS = 14
LEVELS = 24
GASES = 7
FIELD_ROWS = 8 * LEVELS
CLOUD_ROWS = 2 * LEVELS
GAS_ROWS = GASES * LEVELS
PACKED_ROWS = 32
SENT_ROWS = 28
AHEAD = 3
STEPS = 8
TURNS = STEPS + 1
TILES = 16
UNROLL = 24
MESH = pl.DeviceIdType.MESH
SPACE = pltpu.HBM


def split3(x):
    first = x.astype(BF16).astype(F32)
    rest = x - first
    second = rest.astype(BF16).astype(F32)
    return first, second, rest - second


def lane_pad(x):
    return jnp.concatenate([x, jnp.zeros((x.shape[0], LANES - x.shape[1]), F32)], 1)


def make_tables(gas, ray, cloud, solar, surface, snow, coef_ref, solar_ref, albtab_ref):
    shape = (BANDS, LANES)
    band = lax.broadcasted_iota(jnp.int32, shape, 1) // 8 == lax.broadcasted_iota(jnp.int32, shape, 0)
    cloud_gpt = jnp.dot(
        cloud, band.astype(F32), precision=lax.Precision.HIGHEST, preferred_element_type=F32
    )
    ray = lane_pad(ray)
    water, ice = WATER_SSA * cloud_gpt[0:1], ICE_SSA * cloud_gpt[1:2]
    zero6, zero7, zero32 = (jnp.zeros((n, LANES), F32) for n in (6, 7, 32))
    stacks = (
        [lane_pad(gas), ray, cloud_gpt, zero6],
        [zero7, 0.5 * ray, 0.5 * (1 - WATER_ASYM) * water, 0.5 * (1 - ICE_ASYM) * ice, zero6],
        [zero7, 0.5 * ray, 0.5 * (1 + WATER_ASYM) * water, 0.5 * (1 + ICE_ASYM) * ice, zero6],
    )
    for index, stack in enumerate(stacks):
        a1, a2, a3 = split3(jnp.concatenate(stack, 0) * (-DIFFUSIVITY * LOG2E))
        terms = jnp.concatenate([a1, a1, a2, a1, a3, a2, zero32], 0)
        coef_ref[pl.ds(index * GPTS, GPTS), :] = jnp.transpose(terms)[:GPTS].astype(BF16)
    solar = lane_pad(solar)
    solar = solar / jnp.sum(solar)
    square = (LANES, LANES)
    solar_ref[...] = jnp.transpose(jnp.broadcast_to(solar, square))[:GPTS]
    rows = jnp.concatenate([lane_pad(surface), lane_pad(snow)], 0)
    for index in range(5):
        albtab_ref[pl.ds(index * 16, 16), :] = jnp.transpose(
            jnp.broadcast_to(rows[index : index + 1], square)
        )[:16]


def compute_tile(x_ref, state, coef_ref, solar_ref, albtab_ref, alb_ref, layer_ref, net_ref):
    block = (8, LANES)
    kind, share, age, cosine = state[0:1], state[1:2], state[2:3], state[3:4]
    beam_scale = jnp.broadcast_to((1.0 / DIFFUSIVITY) / cosine, block)
    base = jnp.zeros((16, LANES), F32)
    for index in range(4):
        base = jnp.where(kind == float(index), albtab_ref[pl.ds(index * 16, 16), :], base)
    fresh = albtab_ref[pl.ds(64, 16), :] * (1.0 - 0.5 * age)
    alb_ref[...] = (1.0 - share) * base + share * fresh

    def upward(step, carried):
        alb, src = carried
        layer = LEVELS - 1 - step
        x1, x2, x3 = split3(x_ref[pl.ds(layer, 16, stride=LEVELS), :])
        x1, x2, x3 = (part.astype(BF16) for part in (x1, x2, x3))
        terms = jnp.concatenate([x1, x2, x1, x3, x1, x2, jnp.zeros((32, LANES), BF16)], 0)
        optics = jnp.dot(coef_ref[...], terms, preferred_element_type=F32)
        next_alb, next_src = [], []
        for b in range(BANDS):
            depth = optics[8 * b : 8 * b + 8]
            inv_depth = pl.reciprocal(depth, approx=True)
            backward = optics[GPTS + 8 * b : GPTS + 8 * b + 8] * inv_depth
            onward = optics[2 * GPTS + 8 * b : 2 * GPTS + 8 * b + 8] * inv_depth
            diffuse_exp = jnp.exp2(depth)
            beam_exp = jnp.exp2(depth * beam_scale)
            diffuse_loss = 1.0 - diffuse_exp
            beam_loss = 1.0 - beam_exp
            refl_diff = backward * diffuse_loss
            tran_diff = diffuse_exp + onward * diffuse_loss
            refl_dir = backward * beam_loss
            scat_dir = onward * beam_loss
            denom = pl.reciprocal(1.0 - refl_diff * alb[b], approx=True)
            through = tran_diff * denom
            src_beam = src[b] * beam_exp
            gain = (refl_diff * src_beam + scat_dir) * denom
            src_here = refl_dir + through * (src_beam + alb[b] * scat_dir)
            alb_here = refl_diff + tran_diff * through * alb[b]
            layer_ref[layer, 0, b] = through
            layer_ref[layer, 1, b] = gain
            layer_ref[layer, 2, b] = beam_exp
            layer_ref[layer, 3, b] = 1.0 - alb_here
            layer_ref[layer, 4, b] = 1.0 - src_here
            next_alb.append(alb_here)
            next_src.append(src_here)
        return tuple(next_alb), tuple(next_src)

    ground = tuple(jnp.broadcast_to(alb_ref[b : b + 1, :], block) for b in range(BANDS))
    lax.fori_loop(0, LEVELS, upward, (ground, ground), unroll=UNROLL)

    def downward(layer, carried):
        down, direct = carried
        nets, next_down, next_direct = [], [], []
        for b in range(BANDS):
            nets.append(layer_ref[layer, 3, b] * down[b] + layer_ref[layer, 4, b] * direct[b])
            next_down.append(layer_ref[layer, 0, b] * down[b] + layer_ref[layer, 1, b] * direct[b])
            next_direct.append(layer_ref[layer, 2, b] * direct[b])
        while len(nets) > 1:
            nets = [sum(nets[i : i + 2][1:], nets[i]) for i in range(0, len(nets), 2)]
        net_ref[layer] = nets[0]
        return tuple(next_down), tuple(next_direct)

    beam = tuple(solar_ref[pl.ds(8 * b, 8), :] * cosine for b in range(BANDS))
    none = tuple(jnp.zeros(block, F32) for b in range(BANDS))
    down, direct = lax.fori_loop(0, LEVELS, downward, (none, beam), unroll=UNROLL)
    net = jnp.zeros(block, F32)
    for b in range(BANDS):
        net = net + (1.0 - jnp.broadcast_to(alb_ref[b : b + 1, :], block)) * (down[b] + direct[b])
    net_ref[LEVELS] = net
    nets = jnp.sum(net_ref[...], axis=1)
    mass = x_ref[pl.ds(GASES * LEVELS, LEVELS), :]
    return float(LEVELS) * (nets[:LEVELS] - nets[1:]) / mass, nets[LEVELS:]


def kernel(
    gas_hbm, mass_hbm, cloud_hbm, kind_hbm, cover_hbm, age_hbm, cosine_hbm, lit_hbm,
    coeff_hbm, ray_hbm, cext_hbm, surface_hbm, snow_hbm, weight_hbm,
    heat_ref, flux_ref,
    gases, cloud_ref, kind_ref, cover_ref, age_ref, cosine_ref, lit_ref,
    coeff_ref, ray_ref, cext_ref, surface_ref, snow_ref, weight_ref,
    send, recv, heat_out, flux_out, flux_in,
    x_ref, coef_ref, solar_ref, albtab_ref, alb_ref, layer_ref, net_ref,
    load_sem, own_sem, gas_send, gas_recv,
    state_send, state_recv, heat_send, heat_recv, flux_send, flux_recv,
):
    pair, elem = lax.axis_index("pair"), lax.axis_index("elem")
    half_pairs = lax.axis_size("pair") // 2
    side, group = pair // half_pairs, pair % half_pairs
    z, y = elem // 4, elem % 4
    z_block, z_odd, y_pair, y_low = z // 2, z % 2, y // 2, y % 2
    other = 1 - side

    def device(which_side, which_elem):
        return (which_side * half_pairs + group, which_elem)

    partner = device(other, elem)

    def columns(tile):
        return pl.ds(pl.multiple_of(tile * LANES, LANES), LANES)

    def wait_bytes(ref, sem):
        pltpu.make_async_copy(ref, ref, sem).wait()

    def step_tile(step, which_side):
        return 2 * (2 * ((z_block + step // 2) % 4) + which_side) + (y_pair + step % 2) % 2

    def sent_tile(step, z_low):
        z_to = 2 * ((z_block + 4 - step // 2) % 4) + z_low
        return 2 * z_to + (y_pair + step % 2) % 2

    state_loads = [
        pltpu.make_async_copy(source, target, load_sem.at[index])
        for index, (source, target) in enumerate((
            (cloud_hbm, cloud_ref), (kind_hbm, kind_ref), (cover_hbm, cover_ref),
            (age_hbm, age_ref), (cosine_hbm, cosine_ref), (lit_hbm, lit_ref),
        ))
    ]
    table_loads = [
        pltpu.make_async_copy(source, target, load_sem.at[6 + index])
        for index, (source, target) in enumerate((
            (coeff_hbm, coeff_ref), (ray_hbm, ray_ref), (cext_hbm, cext_ref),
            (surface_hbm, surface_ref), (snow_hbm, snow_ref), (weight_hbm, weight_ref),
        ))
    ]
    for copy in state_loads:
        copy.start()

    barrier = pltpu.get_barrier_semaphore()

    def greet(which_side, k):
        pl.semaphore_signal(barrier, inc=1, device_id=device(which_side, k), device_id_type=MESH)

    greet(other, elem)

    def greet_step(step, _):
        for low in range(2):
            for z_low in range(2):
                greet(z_odd, 2 * sent_tile(step, z_low) + low)
            greet(1 - z_odd, 2 * step_tile(step, side) + low)
        return 0

    lax.fori_loop(1, STEPS, greet_step, 0)
    for z_low in range(2):
        for low in range(2):
            near = 2 * sent_tile(0, z_low) + low

            @pl.when(near != elem)
            def _():
                greet(side, near)

    for copy in table_loads:
        copy.start()

    def turn_tile(turn):
        return step_tile(turn % STEPS, jnp.where(turn == STEPS, other, side))

    def load_own(turn, _):
        tile = columns(turn_tile(turn))
        pltpu.make_async_copy(
            gas_hbm.at[:, tile], gases.at[turn, pl.ds(0, GAS_ROWS)], own_sem.at[turn]
        ).start()
        pltpu.make_async_copy(
            mass_hbm.at[:, tile], gases.at[turn, pl.ds(GAS_ROWS, LEVELS)], own_sem.at[turn]
        ).start()
        return 0

    lax.fori_loop(0, TURNS, load_own, 0)

    low_packed = lax.broadcasted_iota(jnp.int32, (PACKED_ROWS, LANES), 1) < HALF
    low8 = lax.broadcasted_iota(jnp.int32, (8, LANES), 1) < HALF

    for copy in state_loads:
        copy.wait()

    def pack_step(step, _):
        for z_low in range(2):
            tile = sent_tile(step, z_low)
            row = pl.ds(tile, 1)
            kind = kind_ref[row, :]
            share = jnp.where(kind >= 1, cover_ref[row, :], 0.0)
            first = jnp.concatenate(
                [
                    cloud_ref[0:LEVELS, columns(tile)], kind.astype(F32), share,
                    age_ref[row, :], cosine_ref[row, :], jnp.zeros((4, LANES), F32),
                ],
                0,
            )
            second = jnp.concatenate(
                [
                    cloud_ref[LEVELS:CLOUD_ROWS, columns(tile)], lit_ref[row, :].astype(F32),
                    jnp.zeros((7, LANES), F32),
                ],
                0,
            )
            send[2 * tile] = jnp.where(low_packed, first, pltpu.roll(second, HALF, 1))
            send[2 * tile + 1] = jnp.where(low_packed, pltpu.roll(first, HALF, 1), second)
        return 0

    lax.fori_loop(0, AHEAD, pack_step, 0)

    pl.semaphore_wait(barrier, 46)

    sent = pl.ds(0, SENT_ROWS)

    def send_near():
        for z_low in range(2):
            for low in range(2):
                k = 2 * sent_tile(0, z_low) + low
                source, target = send.at[k, sent], recv.at[0, z_odd, y_low, sent]

                @pl.when(k != elem)
                def _():
                    pltpu.make_async_remote_copy(
                        src_ref=source, dst_ref=target, send_sem=state_send, recv_sem=state_recv.at[0],
                        device_id=device(side, k), device_id_type=MESH,
                    ).start()

                @pl.when(k == elem)
                def _():
                    pltpu.make_async_copy(source, target, state_recv.at[0]).start()

    def send_step(step, _):
        tile = columns(step_tile(step, other))
        slot = STEPS + step
        for source, target in (
            (gas_hbm.at[:, tile], gases.at[slot, pl.ds(0, GAS_ROWS)]),
            (mass_hbm.at[:, tile], gases.at[slot, pl.ds(GAS_ROWS, LEVELS)]),
        ):
            pltpu.make_async_remote_copy(
                src_ref=source, dst_ref=target, send_sem=gas_send, recv_sem=gas_recv.at[step],
                device_id=partner, device_id_type=MESH,
            ).start()
        for z_low in range(2):
            for low in range(2):
                k = 2 * sent_tile(step, z_low) + low
                pltpu.make_async_remote_copy(
                    src_ref=send.at[k, sent], dst_ref=recv.at[step, side, y_low, sent],
                    send_sem=state_send, recv_sem=state_recv.at[step],
                    device_id=device(z_odd, k), device_id_type=MESH,
                ).start()
        return 0

    send_near()
    lax.fori_loop(1, AHEAD, send_step, 0)
    lax.fori_loop(AHEAD, STEPS, pack_step, 0)
    for copy in table_loads:
        copy.wait()
    make_tables(
        coeff_ref[...], ray_ref[...], cext_ref[...], weight_ref[...], surface_ref[...], snow_ref[...],
        coef_ref, solar_ref, albtab_ref,
    )
    x_ref[pl.ds(10 * LEVELS, 6 * LEVELS), :] = jnp.zeros((6 * LEVELS, LANES), F32)

    def one_tile(turn, _):
        last = turn == STEPS
        step = turn % STEPS
        tile = turn_tile(turn)
        alone = step == 0
        wait_bytes(gases.at[turn], own_sem.at[turn])

        @pl.when(jnp.logical_not(last))
        def _():
            wait_bytes(recv.at[step, :, :, sent], state_recv.at[step])

        @pl.when(jnp.logical_not(alone))
        def _():
            wait_bytes(gases.at[STEPS + step], gas_recv.at[step])

        @pl.when(turn + AHEAD < STEPS)
        def _():
            send_step(turn + AHEAD, 0)

        mine = jnp.where(last, other, side)
        theirs = jnp.where(alone, mine, other)
        own0, own1 = recv[step, mine, 0], recv[step, mine, 1]
        other0, other1 = recv[step, theirs, 0], recv[step, theirs, 1]

        def lit_masks(block0, block1):
            row0, row1 = block0[LEVELS:], block1[LEVELS:]
            turned0, turned1 = pltpu.roll(row0, HALF, 1), pltpu.roll(row1, HALF, 1)
            return (
                jnp.where(low8, turned0, row0)[0:1] > 0.5,
                jnp.where(low8, turned1, row1)[0:1] > 0.5,
                jnp.where(low8, turned0, row1)[0:1] > 0.5,
            )

        mask0, mask1, own_lit = lit_masks(own0, own1)
        other_lit = lit_masks(other0, other1)[2]
        part0 = jnp.where(mask0, own0, other0)
        part1 = jnp.where(mask1, own1, other1)
        first = jnp.where(low_packed, part0, pltpu.roll(part1, HALF, 1))
        second = jnp.where(low_packed, pltpu.roll(part0, HALF, 1), part1)
        x_ref[pl.ds(0, FIELD_ROWS), :] = jnp.where(
            own_lit, gases[turn], gases[jnp.where(alone, turn, STEPS + step)]
        )
        x_ref[pl.ds(FIELD_ROWS, LEVELS), :] = first[0:LEVELS]
        x_ref[pl.ds(FIELD_ROWS + LEVELS, LEVELS), :] = second[0:LEVELS]
        heat, flux = compute_tile(
            x_ref, first[LEVELS:], coef_ref, solar_ref, albtab_ref, alb_ref, layer_ref, net_ref
        )
        for which_side in range(2):
            lit = jnp.where(which_side == side, own_lit.astype(F32), other_lit.astype(F32)) > 0.5
            kept = jnp.broadcast_to(jnp.where(lit, flux, 0.0), (8, LANES))
            flux_out[turn, which_side, 0] = kept[0:1]
            flux_out[turn, which_side, 1] = pltpu.roll(kept, HALF, 1)[0:1]
        for which_side in range(2):
            for low in range(2):
                k = 2 * tile + low
                here = jnp.logical_and(which_side == side, k == elem)
                wanted = jnp.logical_or(which_side == side, jnp.logical_not(alone))
                source, target = flux_out.at[turn, which_side, (low + y_low) % 2], flux_in.at[elem]

                @pl.when(jnp.logical_and(wanted, jnp.logical_not(here)))
                def _():
                    pltpu.make_async_remote_copy(
                        src_ref=source, dst_ref=target, send_sem=flux_send, recv_sem=flux_recv,
                        device_id=device(which_side, k), device_id_type=MESH,
                    ).start()

                @pl.when(here)
                def _():
                    pltpu.make_async_copy(source, target, flux_recv).start()

        @pl.when(jnp.logical_not(alone))
        def _():
            heat_out[step - 1] = jnp.where(other_lit, heat, 0.0)
            pltpu.make_async_remote_copy(
                src_ref=heat_out.at[step - 1], dst_ref=heat_ref.at[:, columns(tile)],
                send_sem=heat_send, recv_sem=heat_recv,
                device_id=partner, device_id_type=MESH,
            ).start()

        heat_ref[:, columns(tile)] = jnp.where(own_lit, heat, 0.0)
        return 0

    lax.fori_loop(0, TURNS, one_tile, 0)

    wait_bytes(gases.at[pl.ds(TURNS, STEPS - 1)], gas_send)
    wait_bytes(send.at[pl.ds(0, 31), sent], state_send)
    wait_bytes(flux_in.at[pl.ds(0, 31)], flux_send)
    wait_bytes(heat_out, heat_send)
    wait_bytes(flux_in, flux_recv)
    for tile in range(TILES):
        flux_ref[tile : tile + 1, :] = jnp.where(low8[0:1], flux_in[2 * tile], flux_in[2 * tile + 1])
    wait_bytes(heat_out, heat_recv)


def body(
    gas_amounts, layer_mass, cloud_paths, surface_kind, snow_cover, snow_age, cos_zenith, sunlit,
    gas_coeff, rayleigh, cloud_ext, surface_table, snow_table, solar_weight,
):
    width = layer_mass.shape[1]
    rows = lambda x: x.reshape(width // LANES, LANES)
    dma = pltpu.SemaphoreType.DMA
    hbm = pl.BlockSpec(memory_space=SPACE)
    vmem = pl.BlockSpec(memory_space=pltpu.VMEM)
    wide = lambda *lead: pltpu.VMEM(lead + (LANES,), F32)
    heating, flux = pl.pallas_call(
        kernel,
        out_shape=(
            jax.ShapeDtypeStruct((LEVELS, width), F32),
            jax.ShapeDtypeStruct((width // LANES, LANES), F32),
        ),
        in_specs=[hbm] * 14,
        out_specs=(vmem, vmem),
        scratch_shapes=[
            wide(2 * STEPS, FIELD_ROWS), pltpu.VMEM((CLOUD_ROWS, width), F32),
            pltpu.VMEM((TILES, LANES), jnp.int32), wide(TILES), wide(TILES), wide(TILES),
            pltpu.VMEM((TILES, LANES), jnp.int32),
            pltpu.VMEM((GASES, GPTS), F32), pltpu.VMEM((1, GPTS), F32), pltpu.VMEM((2, BANDS), F32),
            pltpu.VMEM((4, BANDS), F32), pltpu.VMEM((1, BANDS), F32), pltpu.VMEM((1, GPTS), F32),
            wide(32, PACKED_ROWS), wide(STEPS, 2, 2, PACKED_ROWS),
            wide(STEPS - 1, LEVELS), wide(TURNS, 2, 2, 1), wide(32, 1),
            wide(16 * LEVELS), pltpu.VMEM((3 * GPTS, LANES), BF16), wide(GPTS), wide(80), wide(16),
            wide(LEVELS, 5, BANDS, 8), wide(LEVELS + 1, 8),
            dma((12,)), dma((TURNS,)), dma, dma((STEPS,)),
            dma, dma((STEPS,)), dma, dma, dma, dma,
        ],
        compiler_params=pltpu.CompilerParams(
            collective_id=0, has_side_effects=True, vmem_limit_bytes=60 * 2**20
        ),
    )(
        gas_amounts.reshape(GASES * LEVELS, width),
        layer_mass,
        cloud_paths.reshape(CLOUD_ROWS, width),
        rows(surface_kind), rows(snow_cover), rows(snow_age), rows(cos_zenith), rows(sunlit),
        gas_coeff, rayleigh.reshape(1, GPTS), cloud_ext, surface_table,
        snow_table.reshape(1, BANDS), solar_weight.reshape(1, GPTS),
    )
    return heating, flux.reshape(width)


def solution(mesh):
    columns = ("pair", "elem")
    placed = (
        P(None, None, columns), P(None, columns), P(None, None, columns),
        P(columns), P(columns), P(columns), P(columns), P(columns),
        P(), P(), P(), P(), P(), P(),
    )
    return jax.shard_map(
        body,
        mesh=mesh,
        in_specs=placed,
        out_specs=(P(None, columns), P(columns)),
        check_vma=False,
    )
```

```python
import functools

import jax
import jax.numpy as jnp
from jax import lax
from jax.experimental import pallas as pl
from jax.experimental.pallas import tpu as pltpu
from jax.sharding import PartitionSpec as P

WATER_SSA = 0.999
ICE_SSA = 0.99
WATER_ASYM = 0.85
ICE_ASYM = 0.78
DIFFUSIVITY = 1.66
LOG2E = 1.4426950408889634

F32 = jnp.float32
BF16 = jnp.bfloat16
LANES = 128
HALF = 64
GPTS = 112
BANDS = 14
LEVELS = 24
GASES = 7
FIELD_ROWS = 8 * LEVELS
CLOUD_ROWS = 2 * LEVELS
GAS_ROWS = GASES * LEVELS
PACKED_ROWS = 32
SENT_ROWS = 28
AHEAD = 3
STEPS = 8
TURNS = STEPS + 1
TILES = 16
UNROLL = 24
MESH = pl.DeviceIdType.MESH
SPACE = pltpu.HBM


def split3(x):
    first = x.astype(BF16).astype(F32)
    rest = x - first
    second = rest.astype(BF16).astype(F32)
    return first, second, rest - second


def lane_pad(x):
    return jnp.concatenate([x, jnp.zeros((x.shape[0], LANES - x.shape[1]), F32)], 1)


def make_tables(gas, ray, cloud, solar, surface, snow, coef_ref, solar_ref, albtab_ref):
    shape = (BANDS, LANES)
    band = lax.broadcasted_iota(jnp.int32, shape, 1) // 8 == lax.broadcasted_iota(jnp.int32, shape, 0)
    cloud_gpt = jnp.dot(
        cloud, band.astype(F32), precision=lax.Precision.HIGHEST, preferred_element_type=F32
    )
    ray = lane_pad(ray)
    water, ice = WATER_SSA * cloud_gpt[0:1], ICE_SSA * cloud_gpt[1:2]
    zero6, zero7, zero32 = (jnp.zeros((n, LANES), F32) for n in (6, 7, 32))
    stacks = (
        [lane_pad(gas), ray, cloud_gpt, zero6],
        [zero7, 0.5 * ray, 0.5 * (1 - WATER_ASYM) * water, 0.5 * (1 - ICE_ASYM) * ice, zero6],
        [zero7, 0.5 * ray, 0.5 * (1 + WATER_ASYM) * water, 0.5 * (1 + ICE_ASYM) * ice, zero6],
    )
    for index, stack in enumerate(stacks):
        a1, a2, a3 = split3(jnp.concatenate(stack, 0) * (-DIFFUSIVITY * LOG2E))
        terms = jnp.concatenate([a1, a1, a2, a1, a3, a2, zero32], 0)
        coef_ref[pl.ds(index * GPTS, GPTS), :] = jnp.transpose(terms)[:GPTS].astype(BF16)
    solar = lane_pad(solar)
    solar = solar / jnp.sum(solar)
    square = (LANES, LANES)
    solar_ref[...] = jnp.transpose(jnp.broadcast_to(solar, square))[:GPTS]
    rows = jnp.concatenate([lane_pad(surface), lane_pad(snow)], 0)
    for index in range(5):
        albtab_ref[pl.ds(index * 16, 16), :] = jnp.transpose(
            jnp.broadcast_to(rows[index : index + 1], square)
        )[:16]


def compute_tile(x_ref, state, coef_ref, solar_ref, albtab_ref, alb_ref, layer_ref, net_ref):
    block = (8, LANES)
    kind, share, age, cosine = state[0:1], state[1:2], state[2:3], state[3:4]
    beam_scale = jnp.broadcast_to((1.0 / DIFFUSIVITY) / cosine, block)
    base = jnp.zeros((16, LANES), F32)
    for index in range(4):
        base = jnp.where(kind == float(index), albtab_ref[pl.ds(index * 16, 16), :], base)
    fresh = albtab_ref[pl.ds(64, 16), :] * (1.0 - 0.5 * age)
    alb_ref[...] = (1.0 - share) * base + share * fresh

    def upward(step, carried):
        alb, src = carried
        layer = LEVELS - 1 - step
        x1, x2, x3 = split3(x_ref[pl.ds(layer, 16, stride=LEVELS), :])
        x1, x2, x3 = (part.astype(BF16) for part in (x1, x2, x3))
        terms = jnp.concatenate([x1, x2, x1, x3, x1, x2, jnp.zeros((32, LANES), BF16)], 0)
        optics = jnp.dot(coef_ref[...], terms, preferred_element_type=F32)
        next_alb, next_src = [], []
        for b in range(BANDS):
            depth = optics[8 * b : 8 * b + 8]
            inv_depth = pl.reciprocal(depth, approx=True)
            backward = optics[GPTS + 8 * b : GPTS + 8 * b + 8]
            onward = optics[2 * GPTS + 8 * b : 2 * GPTS + 8 * b + 8]
            diffuse_exp = jnp.exp2(depth)
            beam_exp = jnp.exp2(depth * beam_scale)
            diffuse_loss = (1.0 - diffuse_exp) * inv_depth
            beam_loss = (1.0 - beam_exp) * inv_depth
            refl_diff = backward * diffuse_loss
            tran_diff = diffuse_exp + onward * diffuse_loss
            refl_dir = backward * beam_loss
            scat_dir = onward * beam_loss
            denom = pl.reciprocal(1.0 - refl_diff * alb[b], approx=True)
            through = tran_diff * denom
            src_beam = src[b] * beam_exp
            gain = (refl_diff * src_beam + scat_dir) * denom
            src_here = refl_dir + through * (src_beam + alb[b] * scat_dir)
            alb_here = refl_diff + tran_diff * through * alb[b]
            layer_ref[layer, 0, b] = through
            layer_ref[layer, 1, b] = gain
            layer_ref[layer, 2, b] = beam_exp
            layer_ref[layer, 3, b] = 1.0 - alb_here
            layer_ref[layer, 4, b] = 1.0 - src_here
            next_alb.append(alb_here)
            next_src.append(src_here)
        return tuple(next_alb), tuple(next_src)

    ground = tuple(jnp.broadcast_to(alb_ref[b : b + 1, :], block) for b in range(BANDS))
    lax.fori_loop(0, LEVELS, upward, (ground, ground), unroll=UNROLL)

    def downward(layer, carried):
        down, direct = carried
        net = jnp.zeros(block, F32)
        next_down, next_direct = [], []
        for b in range(BANDS):
            net = net + (layer_ref[layer, 3, b] * down[b] + layer_ref[layer, 4, b] * direct[b])
            next_down.append(layer_ref[layer, 0, b] * down[b] + layer_ref[layer, 1, b] * direct[b])
            next_direct.append(layer_ref[layer, 2, b] * direct[b])
        net_ref[layer] = net
        return tuple(next_down), tuple(next_direct)

    beam = tuple(solar_ref[pl.ds(8 * b, 8), :] * cosine for b in range(BANDS))
    none = tuple(jnp.zeros(block, F32) for b in range(BANDS))
    down, direct = lax.fori_loop(0, LEVELS, downward, (none, beam), unroll=UNROLL // 2)
    net = jnp.zeros(block, F32)
    for b in range(BANDS):
        net = net + (1.0 - jnp.broadcast_to(alb_ref[b : b + 1, :], block)) * (down[b] + direct[b])
    net_ref[LEVELS] = net
    nets = jnp.sum(net_ref[...], axis=1)
    mass = x_ref[pl.ds(GASES * LEVELS, LEVELS), :]
    return float(LEVELS) * (nets[:LEVELS] - nets[1:]) / mass, nets[LEVELS:]


def kernel(
    gas_hbm, mass_hbm, cloud_hbm, kind_hbm, cover_hbm, age_hbm, cosine_hbm, lit_hbm,
    coeff_hbm, ray_hbm, cext_hbm, surface_hbm, snow_hbm, weight_hbm,
    heat_ref, flux_ref,
    gases, cloud_ref, kind_ref, cover_ref, age_ref, cosine_ref, lit_ref,
    coeff_ref, ray_ref, cext_ref, surface_ref, snow_ref, weight_ref,
    send, recv, heat_out, flux_out, flux_in,
    x_ref, coef_ref, solar_ref, albtab_ref, alb_ref, layer_ref, net_ref,
    load_sem, own_sem, gas_send, gas_recv,
    state_send, state_recv, heat_send, heat_recv, flux_send, flux_recv,
):
    pair, elem = lax.axis_index("pair"), lax.axis_index("elem")
    half_pairs = lax.axis_size("pair") // 2
    side, group = pair // half_pairs, pair % half_pairs
    z, y = elem // 4, elem % 4
    z_block, z_odd, y_pair, y_low = z // 2, z % 2, y // 2, y % 2
    other = 1 - side

    def device(which_side, which_elem):
        return (which_side * half_pairs + group, which_elem)

    partner = device(other, elem)

    def columns(tile):
        return pl.ds(pl.multiple_of(tile * LANES, LANES), LANES)

    def wait_bytes(ref, sem):
        pltpu.make_async_copy(ref, ref, sem).wait()

    def step_tile(step, which_side):
        return 2 * (2 * ((z_block + step // 2) % 4) + which_side) + (y_pair + step % 2) % 2

    def sent_tile(step, z_low):
        z_to = 2 * ((z_block + 4 - step // 2) % 4) + z_low
        return 2 * z_to + (y_pair + step % 2) % 2

    state_loads = [
        pltpu.make_async_copy(source, target, load_sem.at[index])
        for index, (source, target) in enumerate((
            (cloud_hbm, cloud_ref), (kind_hbm, kind_ref), (cover_hbm, cover_ref),
            (age_hbm, age_ref), (cosine_hbm, cosine_ref), (lit_hbm, lit_ref),
        ))
    ]
    table_loads = [
        pltpu.make_async_copy(source, target, load_sem.at[6 + index])
        for index, (source, target) in enumerate((
            (coeff_hbm, coeff_ref), (ray_hbm, ray_ref), (cext_hbm, cext_ref),
            (surface_hbm, surface_ref), (snow_hbm, snow_ref), (weight_hbm, weight_ref),
        ))
    ]

    barrier = pltpu.get_barrier_semaphore()

    def greet(which_side, k):
        pl.semaphore_signal(barrier, inc=1, device_id=device(which_side, k), device_id_type=MESH)

    greet(other, elem)

    def greet_step(step, _):
        for low in range(2):
            for z_low in range(2):
                greet(z_odd, 2 * sent_tile(step, z_low) + low)
            greet(1 - z_odd, 2 * step_tile(step, side) + low)
        return 0

    lax.fori_loop(1, STEPS, greet_step, 0)
    for z_low in range(2):
        for low in range(2):
            near = 2 * sent_tile(0, z_low) + low

            @pl.when(near != elem)
            def _():
                greet(side, near)

    for copy in state_loads:
        copy.start()
    for copy in table_loads:
        copy.start()

    def turn_tile(turn):
        return step_tile(turn % STEPS, jnp.where(turn == STEPS, other, side))

    def load_own(turn, _):
        tile = columns(turn_tile(turn))
        pltpu.make_async_copy(
            gas_hbm.at[:, tile], gases.at[turn, pl.ds(0, GAS_ROWS)], own_sem.at[turn]
        ).start()
        pltpu.make_async_copy(
            mass_hbm.at[:, tile], gases.at[turn, pl.ds(GAS_ROWS, LEVELS)], own_sem.at[turn]
        ).start()
        return 0

    load_own(0, 0)

    low_packed = lax.broadcasted_iota(jnp.int32, (PACKED_ROWS, LANES), 1) < HALF
    low8 = lax.broadcasted_iota(jnp.int32, (8, LANES), 1) < HALF

    for copy in state_loads:
        copy.wait()

    def pack_step(step, _):
        for z_low in range(2):
            tile = sent_tile(step, z_low)
            row = pl.ds(tile, 1)
            kind = kind_ref[row, :]
            share = jnp.where(kind >= 1, cover_ref[row, :], 0.0)
            first = jnp.concatenate(
                [
                    cloud_ref[0:LEVELS, columns(tile)], kind.astype(F32), share,
                    age_ref[row, :], cosine_ref[row, :], jnp.zeros((4, LANES), F32),
                ],
                0,
            )
            second = jnp.concatenate(
                [
                    cloud_ref[LEVELS:CLOUD_ROWS, columns(tile)], lit_ref[row, :].astype(F32),
                    jnp.zeros((7, LANES), F32),
                ],
                0,
            )
            send[2 * tile] = jnp.where(low_packed, first, pltpu.roll(second, HALF, 1))
            send[2 * tile + 1] = jnp.where(low_packed, pltpu.roll(first, HALF, 1), second)
        return 0

    pack_step(0, 0)

    pl.semaphore_wait(barrier, 46)

    sent = pl.ds(0, SENT_ROWS)

    def send_near():
        for z_low in range(2):
            for low in range(2):
                k = 2 * sent_tile(0, z_low) + low
                source, target = send.at[k, sent], recv.at[0, z_odd, y_low, sent]

                @pl.when(k != elem)
                def _():
                    pltpu.make_async_remote_copy(
                        src_ref=source, dst_ref=target, send_sem=state_send, recv_sem=state_recv.at[0],
                        device_id=device(side, k), device_id_type=MESH,
                    ).start()

                @pl.when(k == elem)
                def _():
                    pltpu.make_async_copy(source, target, state_recv.at[0]).start()

    def send_step(step, _):
        tile = columns(step_tile(step, other))
        slot = STEPS + step
        for source, target in (
            (gas_hbm.at[:, tile], gases.at[slot, pl.ds(0, GAS_ROWS)]),
            (mass_hbm.at[:, tile], gases.at[slot, pl.ds(GAS_ROWS, LEVELS)]),
        ):
            pltpu.make_async_remote_copy(
                src_ref=source, dst_ref=target, send_sem=gas_send, recv_sem=gas_recv.at[step],
                device_id=partner, device_id_type=MESH,
            ).start()
        for z_low in range(2):
            for low in range(2):
                k = 2 * sent_tile(step, z_low) + low
                pltpu.make_async_remote_copy(
                    src_ref=send.at[k, sent], dst_ref=recv.at[step, side, y_low, sent],
                    send_sem=state_send, recv_sem=state_recv.at[step],
                    device_id=device(z_odd, k), device_id_type=MESH,
                ).start()
        return 0

    send_near()

    def pack_and_send(step, _):
        pack_step(step, 0)
        return send_step(step, 0)

    lax.fori_loop(1, AHEAD, pack_and_send, 0)
    lax.fori_loop(1, TURNS, load_own, 0)
    lax.fori_loop(AHEAD, STEPS, pack_step, 0)
    for copy in table_loads:
        copy.wait()
    make_tables(
        coeff_ref[...], ray_ref[...], cext_ref[...], weight_ref[...], surface_ref[...], snow_ref[...],
        coef_ref, solar_ref, albtab_ref,
    )
    x_ref[pl.ds(10 * LEVELS, 6 * LEVELS), :] = jnp.zeros((6 * LEVELS, LANES), F32)

    def one_tile(turn, _):
        last = turn == STEPS
        step = turn % STEPS
        tile = turn_tile(turn)
        alone = step == 0
        wait_bytes(gases.at[turn], own_sem.at[turn])

        @pl.when(jnp.logical_not(last))
        def _():
            wait_bytes(recv.at[step, :, :, sent], state_recv.at[step])

        @pl.when(jnp.logical_not(alone))
        def _():
            wait_bytes(gases.at[STEPS + step], gas_recv.at[step])

        @pl.when(turn + AHEAD < STEPS)
        def _():
            send_step(turn + AHEAD, 0)

        mine = jnp.where(last, other, side)
        theirs = jnp.where(alone, mine, other)
        own0, own1 = recv[step, mine, 0], recv[step, mine, 1]
        other0, other1 = recv[step, theirs, 0], recv[step, theirs, 1]

        def lit_masks(block0, block1):
            row0, row1 = block0[LEVELS:], block1[LEVELS:]
            turned0, turned1 = pltpu.roll(row0, HALF, 1), pltpu.roll(row1, HALF, 1)
            return (
                jnp.where(low8, turned0, row0)[0:1] > 0.5,
                jnp.where(low8, turned1, row1)[0:1] > 0.5,
                jnp.where(low8, turned0, row1)[0:1] > 0.5,
            )

        mask0, mask1, own_lit = lit_masks(own0, own1)
        other_lit = lit_masks(other0, other1)[2]
        part0 = jnp.where(mask0, own0, other0)
        part1 = jnp.where(mask1, own1, other1)
        first = jnp.where(low_packed, part0, pltpu.roll(part1, HALF, 1))
        second = jnp.where(low_packed, pltpu.roll(part0, HALF, 1), part1)
        x_ref[pl.ds(0, FIELD_ROWS), :] = jnp.where(
            own_lit, gases[turn], gases[jnp.where(alone, turn, STEPS + step)]
        )
        x_ref[pl.ds(FIELD_ROWS, LEVELS), :] = first[0:LEVELS]
        x_ref[pl.ds(FIELD_ROWS + LEVELS, LEVELS), :] = second[0:LEVELS]
        heat, flux = compute_tile(
            x_ref, first[LEVELS:], coef_ref, solar_ref, albtab_ref, alb_ref, layer_ref, net_ref
        )
        for which_side in range(2):
            lit = jnp.where(which_side == side, own_lit.astype(F32), other_lit.astype(F32)) > 0.5
            kept = jnp.broadcast_to(jnp.where(lit, flux, 0.0), (8, LANES))
            flux_out[turn, which_side, 0] = kept[0:1]
            flux_out[turn, which_side, 1] = pltpu.roll(kept, HALF, 1)[0:1]
        def flux_copy(which_side, low):
            return pltpu.make_async_remote_copy(
                src_ref=flux_out.at[turn, which_side, (low + y_low) % 2], dst_ref=flux_in.at[elem],
                send_sem=flux_send, recv_sem=flux_recv,
                device_id=device(which_side, 2 * tile + low), device_id_type=MESH,
            )

        @pl.when(alone)
        def _():
            for low in range(2):
                here = 2 * tile + low == elem

                @pl.when(jnp.logical_not(here))
                def _():
                    flux_copy(side, low).start()

                @pl.when(here)
                def _():
                    pltpu.make_async_copy(
                        flux_out.at[turn, side, (low + y_low) % 2], flux_in.at[elem], flux_recv
                    ).start()

        @pl.when(jnp.logical_not(alone))
        def _():
            heat_out[step - 1] = jnp.where(other_lit, heat, 0.0)
            pltpu.make_async_remote_copy(
                src_ref=heat_out.at[step - 1], dst_ref=heat_ref.at[:, columns(tile)],
                send_sem=heat_send, recv_sem=heat_recv,
                device_id=partner, device_id_type=MESH,
            ).start()
            for which_side in range(2):
                for low in range(2):
                    flux_copy(which_side, low).start()

        heat_ref[:, columns(tile)] = jnp.where(own_lit, heat, 0.0)
        return 0

    lax.fori_loop(0, TURNS, one_tile, 0)

    wait_bytes(gases.at[pl.ds(TURNS, STEPS - 1)], gas_send)
    wait_bytes(send.at[pl.ds(0, 31), sent], state_send)
    wait_bytes(flux_in.at[pl.ds(0, 31)], flux_send)
    wait_bytes(heat_out, heat_send)
    wait_bytes(flux_in, flux_recv)
    for tile in range(TILES):
        flux_ref[tile : tile + 1, :] = jnp.where(low8[0:1], flux_in[2 * tile], flux_in[2 * tile + 1])
    wait_bytes(heat_out, heat_recv)


def body(
    gas_amounts, layer_mass, cloud_paths, surface_kind, snow_cover, snow_age, cos_zenith, sunlit,
    gas_coeff, rayleigh, cloud_ext, surface_table, snow_table, solar_weight,
):
    width = layer_mass.shape[1]
    rows = lambda x: x.reshape(width // LANES, LANES)
    dma = pltpu.SemaphoreType.DMA
    hbm = pl.BlockSpec(memory_space=SPACE)
    vmem = pl.BlockSpec(memory_space=pltpu.VMEM)
    wide = lambda *lead: pltpu.VMEM(lead + (LANES,), F32)
    heating, flux = pl.pallas_call(
        kernel,
        out_shape=(
            jax.ShapeDtypeStruct((LEVELS, width), F32),
            jax.ShapeDtypeStruct((width // LANES, LANES), F32),
        ),
        in_specs=[hbm] * 14,
        out_specs=(vmem, vmem),
        scratch_shapes=[
            wide(2 * STEPS, FIELD_ROWS), pltpu.VMEM((CLOUD_ROWS, width), F32),
            pltpu.VMEM((TILES, LANES), jnp.int32), wide(TILES), wide(TILES), wide(TILES),
            pltpu.VMEM((TILES, LANES), jnp.int32),
            pltpu.VMEM((GASES, GPTS), F32), pltpu.VMEM((1, GPTS), F32), pltpu.VMEM((2, BANDS), F32),
            pltpu.VMEM((4, BANDS), F32), pltpu.VMEM((1, BANDS), F32), pltpu.VMEM((1, GPTS), F32),
            wide(32, PACKED_ROWS), wide(STEPS, 2, 2, PACKED_ROWS),
            wide(STEPS - 1, LEVELS), wide(TURNS, 2, 2, 1), wide(32, 1),
            wide(16 * LEVELS), pltpu.VMEM((3 * GPTS, LANES), BF16), wide(GPTS), wide(80), wide(16),
            wide(LEVELS, 5, BANDS, 8), wide(LEVELS + 1, 8),
            dma((12,)), dma((TURNS,)), dma, dma((STEPS,)),
            dma, dma((STEPS,)), dma, dma, dma, dma,
        ],
        compiler_params=pltpu.CompilerParams(
            collective_id=0, has_side_effects=True, vmem_limit_bytes=60 * 2**20
        ),
    )(
        gas_amounts.reshape(GASES * LEVELS, width),
        layer_mass,
        cloud_paths.reshape(CLOUD_ROWS, width),
        rows(surface_kind), rows(snow_cover), rows(snow_age), rows(cos_zenith), rows(sunlit),
        gas_coeff, rayleigh.reshape(1, GPTS), cloud_ext, surface_table,
        snow_table.reshape(1, BANDS), solar_weight.reshape(1, GPTS),
    )
    return heating, flux.reshape(width)


def solution(mesh):
    columns = ("pair", "elem")
    placed = (
        P(None, None, columns), P(None, columns), P(None, None, columns),
        P(columns), P(columns), P(columns), P(columns), P(columns),
        P(), P(), P(), P(), P(), P(),
    )
    return jax.shard_map(
        body,
        mesh=mesh,
        in_specs=placed,
        out_specs=(P(None, columns), P(columns)),
        check_vma=False,
    )
```
